256 devices in a mesh: pair: 32 (over z, x), row: 8 (over y, core).
Axes of the slice: x: 4, y: 4, z: 8, core: 2. Of those that a mesh axis runs over, the one named last changes fastest.
Arguments:
- features: bfloat16 [64, 8, 32, 1024], P('pair', 'row'), may hold values from -6 to 6
- src_ids: int32 [64], replicated, may hold values from 0 to 63
- tgt_ids: int32 [64], replicated, may hold values from 0 to 63
- image_slot: int32 [64], replicated, may hold values from 0 to 63, each once
- w_first: bfloat16 [81, 16, 1], replicated, may hold values from -0.625 to 0.625
- w_mid: bfloat16 [81, 16, 16], replicated, may hold values from -0.15625 to 0.15625
- w_last: bfloat16 [81, 1, 16], replicated, may hold values from -0.15625 to 0.15625
Outputs:
- matches: bfloat16 [64, 8, 32, 256], P('pair', 'row')
The draws below stay inside these ranges and needn't reach their ends.
All inputs are finite; a program needn't handle non-finite values.
Results may differ from the reference program's by a relative error of at most 0.012.
The reference program's roundings to bfloat16 on the way (of `normed`, `correlation`, `hidden_one` and `hidden_two`) count: a program that leaves them out, or rounds other values in their place, can miss the bound.
Values may be sent and summed in bfloat16 or wider, within the bound.
No kernel may reach another device: no remote copies, remote signals or barrier semaphores. Data moves between devices by JAX's collectives and lax.ppermute only.
A program may use at most 64 MiB of HBM per device.

```python
import math
import jax
import jax.numpy as jnp
import numpy as np
from jax import lax

FEAT = 1024
CONV = 16
WID = 32
HGT = 8
IMAGES = 64
PAIRS = 64


def place_ends(drawn, own_key, smallest, top_value):
    spot = [jax.random.randint(jax.random.fold_in(own_key, axis), (), 0, length) for axis, length in enumerate(drawn.shape)]
    longest = drawn.shape.index(max(drawn.shape))
    beside = spot[:longest] + [(spot[longest] + 1) % drawn.shape[longest]] + spot[longest + 1:]
    return drawn.at[tuple(spot)].set(smallest).at[tuple(beside)].set(top_value)


def levels(key, extent, split, least, top_value):
    gain = 1.0
    for axis_at, parts in split:
        draws = jax.random.uniform(jax.random.fold_in(jax.random.fold_in(key, 6), axis_at), (parts,), jnp.float32, least / len(split), top_value / len(split))
        gain = gain * jnp.repeat(jnp.exp(draws), extent[axis_at] // parts).reshape((-1,) + (1,) * (len(extent) - 1 - axis_at))
    return gain


def rank_bounds(number_of, skew):
    portions = [(1 << 20) // math.isqrt(rank ** skew) + 1 for rank in range(1, number_of + 1)]
    spread = 1 + sum(portions) // (1 << 30)
    return np.cumsum(np.array([max(1, weight // spread) for weight in portions]))


def skewed_ids(own_key, extent, number_of, lean):
    grid = rank_bounds(number_of, lean)
    lot = jax.random.randint(jax.random.fold_in(own_key, 1), extent, 0, int(grid[number_of - 1]))
    grade = jnp.searchsorted(jnp.asarray(grid, jnp.int32), lot, side="right")
    return jax.random.permutation(jax.random.fold_in(own_key, 2), number_of)[grade].astype(jnp.int32)


def gaussian(rng, shape, spread, most, cuts=(), kind=jnp.bfloat16):
    entries = spread * jax.random.normal(rng, shape, jnp.float32)
    if cuts:
        entries = entries * levels(rng, shape, cuts, -0.22, 0.18)
    return jnp.clip(entries, -most, most).astype(kind)


def setup_inputs(seed: int = 0) -> dict:
    streams_of = jax.random.split(jax.random.key(seed), 8)
    return {
        "features": gaussian(streams_of[0], (IMAGES, HGT, WID, FEAT), 1.0, 6.0, ((0, 32), (1, 8))),
        "src_ids": place_ends(skewed_ids(streams_of[1], (PAIRS,), IMAGES, 2), jax.random.fold_in(streams_of[1], 3), 0, IMAGES - 1).astype(jnp.int32),
        "tgt_ids": place_ends(skewed_ids(streams_of[2], (PAIRS,), IMAGES, 1), jax.random.fold_in(streams_of[2], 3), 0, IMAGES - 1).astype(jnp.int32),
        "image_slot": jax.random.permutation(streams_of[3], IMAGES).astype(jnp.int32),
        "w_first": gaussian(streams_of[4], (81, CONV, 1), 81 ** -0.5, 0.625),
        "w_mid": gaussian(streams_of[5], (81, CONV, CONV), (81 * CONV) ** -0.5, 0.15625),
        "w_last": gaussian(streams_of[6], (81, 1, CONV), (81 * CONV) ** -0.5, 0.15625),
    }


EPSILON = 1e-05
NORM_EPS = 1e-06

def normalize(features):
    flattened = features.astype(jnp.float32)
    scale = lax.rsqrt(lax.optimization_barrier(jnp.sum(flattened * flattened, axis=-1, keepdims=True)) + NORM_EPS)
    return (flattened * scale).astype(jnp.bfloat16)

def consensus_layer(tensor, weight, is_last):
    channels_in = tensor.shape[0]
    channels_out = weight.shape[1]
    kernels = weight.astype(jnp.float32).reshape(3, 3, 3, 3, channels_out, channels_in)
    padded = jnp.pad(tensor.astype(jnp.float32), ((0, 0), (1, 1), (0, 0), (0, 0), (0, 0)))
    summed = jnp.zeros((HGT, channels_out, WID, HGT, WID), jnp.float32)
    for a in range(3):
        window = jnp.transpose(padded[:, a:a + HGT], (1, 0, 2, 3, 4))
        kernel = jnp.transpose(kernels[a], (3, 4, 0, 1, 2))
        summed = summed + lax.conv_general_dilated(window, kernel, (1, 1, 1), 'SAME', precision=lax.Precision.HIGHEST)
    result = jax.nn.relu(jnp.transpose(summed, (1, 0, 2, 3, 4)))
    if is_last:
        return result
    return result.astype(jnp.bfloat16)

def reference(features, src_ids, tgt_ids, image_slot, w_first, w_mid, w_last):
    normed = normalize(features)
    positions = HGT * WID

    def one_pair(pair_ids):
        source = normed[image_slot[pair_ids[0]]].reshape(positions, FEAT)
        target = normed[image_slot[pair_ids[1]]].reshape(positions, FEAT)
        correlation = jnp.dot(source, target.T, preferred_element_type=jnp.float32).astype(jnp.bfloat16)
        correlation = correlation.reshape(1, HGT, WID, HGT, WID)
        hidden_one = consensus_layer(correlation, w_first, False)
        hidden_two = consensus_layer(hidden_one, w_mid, False)
        consensus = consensus_layer(hidden_two, w_last, True)[0]
        source_best = lax.optimization_barrier(jnp.max(consensus, axis=(0, 1)))
        target_best = lax.optimization_barrier(jnp.max(consensus, axis=(2, 3), keepdims=True))
        matches = consensus / (source_best + EPSILON) * (consensus / (target_best + EPSILON))
        return matches.astype(jnp.bfloat16).reshape(HGT, WID, positions)
    return lax.map(one_pair, jnp.stack([src_ids, tgt_ids], axis=1))
```

```python
import functools

import jax
import jax.numpy as jnp
from jax import lax
from jax.experimental import pallas as pl
from jax.experimental.pallas import tpu as pltpu
from jax.sharding import PartitionSpec as P

WID = 32
HGT = 8
POS = HGT * WID
CONV = 16
EPSILON = 1e-05
NORM_EPS = 1e-06
BF16 = jnp.bfloat16
F32 = jnp.float32

CHIPS = 4
BLOCK = WID // CHIPS
COLS_IN, COLS_1, COLS_2 = BLOCK + 8, BLOCK + 4, BLOCK + 2
HALF = COLS_2 // 2
ROWS_1, ROWS_2 = COLS_1 * CONV, COLS_2 * CONV
K_1 = 27 * COLS_IN
K_PIECE = (HALF + 2) * CONV
K_2 = 9 * K_PIECE
M_2 = HALF * CONV


def whole(space=pltpu.VMEM):
    return pl.BlockSpec(memory_space=space)


def call(kernel, out_shape, inputs, scalars=(), scratch=()):
    return pl.pallas_call(
        kernel,
        out_shape=out_shape,
        in_specs=[whole(pltpu.SMEM)] * len(scalars) + [whole()] * len(inputs),
        out_specs=jax.tree.map(lambda _: whole(), out_shape),
        scratch_shapes=list(scratch),
        compiler_params=pltpu.CompilerParams(vmem_limit_bytes=40 * 1024 * 1024),
    )(*scalars, *inputs)


def spread_kernel(core_ref, own_ref, other_ref, out_ref, rows_ref):
    core = core_ref[0]
    images = own_ref.shape[0]
    for ref, place in ((own_ref, core), (other_ref, 1 - core)):
        for image in range(images):
            cells = ref[image, 0].astype(F32)
            scale = lax.rsqrt(jnp.sum(cells * cells, axis=-1, keepdims=True) + NORM_EPS)
            rows_ref[place, image] = (cells * scale).astype(BF16)
    for row in range(2):
        for half in range(2):
            for block in range(8):
                for image in range(images):
                    out_ref[(row * 2 + half) * 8 + block, image] = rows_ref[
                        row, image, half * 16 : half * 16 + 16, block * 128 : block * 128 + 128
                    ]


def select_kernel(core_ref, src_ref, tgt_ref, slot_ref, held_ref, out_ref):
    core = core_ref[0]
    for group in range(out_ref.shape[0]):
        pair = 2 * group + core
        out_ref[group, 0] = held_ref[slot_ref[src_ref[pair]]]
        out_ref[group, 1] = held_ref[slot_ref[tgt_ref[pair]]]


def pack_kernel(chip_ref, held_ref, out_0, out_1, out_2, out_3, windows_ref):
    chip = chip_ref[0]
    for row in range(2):
        for block in range(8):
            left = held_ref[row * 16 + block, 0].astype(F32)
            right = held_ref[row * 16 + 8 + block, 0].astype(F32)
            edge = jnp.zeros((4, 128), F32)
            line = jnp.concatenate([edge, left, right, edge], axis=0)
            for y in range(CHIPS):
                windows_ref[y, row * 8 + block] = line[y * BLOCK : y * BLOCK + 16].astype(BF16)
    for step, out_ref in enumerate((out_0, out_1, out_2, out_3)):
        for tile in range(32):
            out_ref[tile] = held_ref[tile, 1]
        out_ref[32:48] = windows_ref[lax.rem(chip + step, CHIPS)]


def shifted(values, offset):
    amount = (-offset) % POS
    return pltpu.roll(values, amount, values.ndim - 1) if amount else values


def consensus_kernel(
    chip_ref, got_0, got_1, got_2, got_3, z1_ref, z2_ref, z3_ref, out_ref, src, tgt, x1, x2, h2, w3s
):
    chip = chip_ref[0]
    for step, got in enumerate((got_0, got_1, got_2, got_3)):
        origin = lax.rem(chip + CHIPS - step, CHIPS)
        for quarter in range(4):
            rows = pl.ds(pl.multiple_of(origin * 64 + quarter * 16, 16), 16)
            for block in range(8):
                tgt[rows, block * 128 : block * 128 + 128] = got[quarter * 8 + block]
        for row in range(2):
            rows = pl.ds(pl.multiple_of(origin * 32 + row * 16, 16), 16)
            for block in range(8):
                src[rows, block * 128 : block * 128 + 128] = got[32 + row * 8 + block]
    corr = lax.dot_general(src[...], tgt[...], (((1,), (1,)), ((), ())), preferred_element_type=F32)
    corr = corr.astype(BF16).astype(F32)

    column = lax.broadcasted_iota(jnp.int32, (1, POS), 1)
    line = column // WID
    column = column % WID

    def col_mask(d):
        return ((column + d - 1 >= 0) & (column + d - 1 < WID)).astype(F32)

    def line_mask(c):
        return ((line + c - 1 >= 0) & (line + c - 1 < HGT)).astype(F32)

    has_left = (chip > 0).astype(F32)
    has_right = (chip < CHIPS - 1).astype(F32)

    z1 = z1_ref[...].astype(F32)
    w1 = jnp.concatenate([pltpu.roll(z1, j, 1) if j else z1 for j in range(COLS_1)], axis=0).astype(BF16)[:, :K_1]
    z2 = z2_ref[...].astype(F32)
    rolled = [pltpu.roll(z2, CONV * j, 1) if j else z2 for j in range(HALF)]
    w2 = jnp.concatenate(
        [rolled[j][c * CONV : c * CONV + CONV] for c in range(3) for j in range(HALF)], axis=0
    ).astype(BF16)[:, :K_2]
    z3 = z3_ref[...].astype(F32)
    for j in range(BLOCK):
        w3s[:, j, :] = pltpu.roll(z3, CONV * j, 1) if j else z3
    w3 = w3s[...].reshape(27 * BLOCK, 256).astype(BF16)[:, :ROWS_2]

    for c in range(3):
        for d in range(3):
            moved = shifted(corr, WID * (c - 1) + d - 1) * (line_mask(c) * col_mask(d))
            x1[c * 3 + d, 0:16] = jnp.zeros((16, POS), BF16)
            x1[c * 3 + d, 16 : 16 + 128] = moved.astype(BF16)
            x1[c * 3 + d, 144:160] = jnp.zeros((16, POS), BF16)
    for d in range(3):
        x2[d, 0:ROWS_1] = jnp.zeros((ROWS_1, POS), BF16)
        x2[d, (HGT + 1) * ROWS_1 :] = jnp.zeros((ROWS_1, POS), BF16)
    left_mask, right_mask = col_mask(0), col_mask(2)
    for i in range(HGT):
        cells = jnp.concatenate([x1[k, 16 * i : 16 * i + 48] for k in range(9)], axis=0)
        hidden = jnp.maximum(jnp.dot(w1, cells, preferred_element_type=F32), 0.0)
        edge = 2 * CONV
        hidden = jnp.concatenate(
            [hidden[:edge] * has_left, hidden[edge : ROWS_1 - edge], hidden[ROWS_1 - edge :] * has_right], axis=0
        )
        at = (i + 1) * ROWS_1
        x2[0, at : at + ROWS_1] = (shifted(hidden, -1) * left_mask).astype(BF16)
        x2[1, at : at + ROWS_1] = hidden.astype(BF16)
        x2[2, at : at + ROWS_1] = (shifted(hidden, 1) * right_mask).astype(BF16)

    up_mask, down_mask = line_mask(0), line_mask(2)
    for i in range(HGT):
        for half in range(2):
            first = half * HALF * CONV
            cells = jnp.concatenate(
                [x2[d, (i + a) * ROWS_1 + first : (i + a) * ROWS_1 + first + K_PIECE] for d in range(3) for a in range(3)],
                axis=0,
            )
            parts = jnp.dot(w2, cells, preferred_element_type=F32)
            total = parts[M_2 : 2 * M_2]
            total = total + shifted(parts[:M_2], -WID) * up_mask
            total = total + shifted(parts[2 * M_2 :], WID) * down_mask
            total = jnp.maximum(total, 0.0)
            if half == 0:
                total = jnp.concatenate([total[:CONV] * has_left, total[CONV:]], axis=0)
            else:
                total = jnp.concatenate([total[: M_2 - CONV], total[M_2 - CONV :] * has_right], axis=0)
            h2[i, first : first + M_2] = total.astype(BF16)

    sums = [None] * HGT
    for i in range(HGT):
        parts = jnp.dot(w3, h2[i], preferred_element_type=F32)
        for a in range(3):
            o = i + 1 - a
            if 0 <= o < HGT:
                part = parts[a * 9 * BLOCK : (a + 1) * 9 * BLOCK]
                sums[o] = part if sums[o] is None else sums[o] + part
    best = None
    scores = []
    for i in range(HGT):
        total = None
        for c in range(3):
            for d in range(3):
                k = (c * 3 + d) * BLOCK
                part = shifted(sums[i][k : k + BLOCK], WID * (c - 1) + d - 1) * (line_mask(c) * col_mask(d))
                total = part if total is None else total + part
        total = jnp.maximum(total, 0.0)
        top = jnp.max(total, axis=0, keepdims=True)
        best = top if best is None else jnp.maximum(best, top)
        target_best = jnp.max(total, axis=1, keepdims=True)
        scores.append(total * (total / (target_best + EPSILON)))
    pieces = []
    rest = best
    for _ in range(3):
        piece = rest.astype(BF16).astype(F32)
        pieces.append(piece)
        rest = rest - piece
    pieces.append(jnp.zeros((5, POS), F32))
    pieces = jnp.concatenate(pieces, axis=0)
    for i in range(HGT):
        out_ref[i] = jnp.concatenate([scores[i], pieces], axis=0).astype(BF16)


def finish_kernel(got_ref, out_ref):
    for pair in range(2):
        best = None
        for chip in range(CHIPS):
            top = got_ref[2 * chip + pair].astype(F32)
            top = top[8:9] + top[9:10] + top[10:11]
            best = top if best is None else jnp.maximum(best, top)
        best = best + EPSILON
        lines = [got_ref[2 * chip + pair].astype(F32)[:8] / best for chip in range(CHIPS)]
        out_ref[pair, 0] = jnp.concatenate(lines, axis=0).astype(BF16)


def row_moves(chips, cores):
    return [(2 * y + c, 2 * ((y + chips) % CHIPS) + (c ^ cores)) for y in range(CHIPS) for c in range(2)]


def local(features, src_ids, tgt_ids, image_slot, w_first, w_mid, w_last):
    groups = lax.axis_size("pair")
    images, _, _, channels = features.shape
    place = lax.axis_index("row").astype(jnp.int32)
    chip = (place // 2).reshape(1)
    core = (place % 2).reshape(1)

    taps = w_first.reshape(3, 3, 3, 3, CONV).transpose(4, 2, 3, 0, 1)
    z1 = jnp.pad(taps, ((0, 0),) * 4 + ((1, COLS_IN - 4),)).reshape(CONV, K_1)
    z1 = jnp.pad(z1, ((0, 0), (0, 512 - K_1)))
    taps = w_mid.reshape(3, 3, 3, 3, CONV, CONV).transpose(2, 4, 3, 0, 1, 5)
    z2 = jnp.pad(taps, ((0, 0),) * 4 + ((0, HALF - 1), (0, 0))).reshape(3 * CONV, K_2)
    z2 = jnp.pad(z2, ((0, 0), (0, 1024 - K_2)))
    z3 = w_last.reshape(3, 3, 3, 3, CONV).transpose(0, 2, 3, 1, 4).reshape(27, 3 * CONV)
    z3 = jnp.pad(z3, ((0, 0), (0, 256 - 3 * CONV)))

    other = lax.ppermute(features, "row", row_moves(0, 1))
    tiles = call(
        spread_kernel,
        jax.ShapeDtypeStruct((groups, images, 16, 128), BF16),
        (features, other),
        (core,),
        (pltpu.VMEM((2, images, WID, channels), BF16),),
    )
    held = lax.all_to_all(tiles, "pair", 0, 0, tiled=True).reshape(groups * images, 16, 128)
    wanted = call(
        select_kernel,
        jax.ShapeDtypeStruct((groups, 2, 16, 128), BF16),
        (held,),
        (core, src_ids, tgt_ids, image_slot),
    )
    routed = lax.all_to_all(wanted, "pair", 0, 0, tiled=True)
    message = jax.ShapeDtypeStruct((48, 16, 128), BF16)
    sends = call(
        pack_kernel, (message,) * 4, (routed,), (chip,), (pltpu.VMEM((CHIPS, 16, 16, 128), BF16),)
    )
    gots = [sends[0]] + [lax.ppermute(sends[k], "row", row_moves(k, 0)) for k in range(1, CHIPS)]
    scores = call(
        consensus_kernel,
        jax.ShapeDtypeStruct((HGT, 16, POS), BF16),
        (*gots, z1, z2, z3),
        (chip,),
        (
            pltpu.VMEM((HGT * COLS_IN, channels), BF16),
            pltpu.VMEM((POS, channels), BF16),
            pltpu.VMEM((9, 160, POS), BF16),
            pltpu.VMEM((3, (HGT + 2) * ROWS_1, POS), BF16),
            pltpu.VMEM((HGT, ROWS_2, POS), BF16),
            pltpu.VMEM((27, BLOCK, 256), F32),
        ),
    )
    swapped = lax.all_to_all(scores, "row", 0, 0, tiled=True)
    return call(finish_kernel, jax.ShapeDtypeStruct((2, 1, WID, POS), BF16), (swapped,))


def solution(mesh):
    placed = (P("pair", "row", None, None), P(), P(), P(), P(), P(), P())
    return jax.shard_map(
        local, mesh=mesh, in_specs=placed, out_specs=P("pair", "row", None, None), check_vma=False
    )
```

```python
import jax
import jax.numpy as jnp
from jax import lax
from jax.experimental import pallas as pl
from jax.experimental.pallas import tpu as pltpu
from jax.sharding import PartitionSpec as P

WID = 32
HGT = 8
POS = HGT * WID
CONV = 16
EPSILON = 1e-05
NORM_EPS = 1e-06
BF16 = jnp.bfloat16
F32 = jnp.float32

CHIPS = 4
BLOCK = WID // 2
COLS_IN = 16
PART_1 = 10
COLS_1, COLS_2 = BLOCK + 4, BLOCK + 2
PART_2 = 6
PART_3 = 8
ROWS_1, ROWS_2 = COLS_1 * CONV, COLS_2 * CONV
K_1 = 27 * COLS_IN
K_PIECE = (PART_2 + 2) * CONV
K_2 = 9 * K_PIECE
M_1 = PART_1 * CONV
M_2 = PART_2 * CONV
K_3 = (PART_3 + 2) * CONV
FRAME = WID + 16


def whole(space=pltpu.VMEM):
    return pl.BlockSpec(memory_space=space)


def call(kernel, out_shape, inputs, scalars=(), scratch=(), out_specs=None):
    return pl.pallas_call(
        kernel,
        out_shape=out_shape,
        in_specs=[whole(pltpu.SMEM)] * len(scalars) + [whole()] * len(inputs),
        out_specs=jax.tree.map(lambda _: whole(), out_shape) if out_specs is None else out_specs,
        scratch_shapes=list(scratch),
        compiler_params=pltpu.CompilerParams(vmem_limit_bytes=48 * 1024 * 1024),
    )(*scalars, *inputs)


def spread_kernel(src_ref, tgt_ref, slot_ref, own_ref, out_ref, slots_ref):
    for pair in range(src_ref.shape[0]):
        slots_ref[2 * pair] = slot_ref[src_ref[pair]]
        slots_ref[2 * pair + 1] = slot_ref[tgt_ref[pair]]
    rows = []
    for image in range(2):
        cells = own_ref[image, 0].astype(F32)
        scale = lax.rsqrt(jnp.sum(cells * cells, axis=-1, keepdims=True) + NORM_EPS)
        rows.append(cells * scale)
    for part in range(4):
        for block in range(8):
            at = slice(part * 8, part * 8 + 8), slice(block * 128, block * 128 + 128)
            out_ref[part * 8 + block] = jnp.concatenate([rows[0][at], rows[1][at]], axis=0).astype(BF16)


def select_kernel(slots_ref, held_ref, out_ref, pieces):
    groups = held_ref.shape[0]
    for group in range(groups):
        both = held_ref[group].astype(F32)
        pieces[2 * group] = both[:8]
        pieces[2 * group + 1] = both[8:]
    for group in range(groups):
        for pair in range(2):
            at = 4 * group + 2 * pair
            out_ref[group, pair] = jnp.concatenate(
                [pieces[slots_ref[at]], pieces[slots_ref[at + 1]]], axis=0
            ).astype(BF16)


def pack_kernel(chip_ref, held_ref, out_0, out_1, out_2, out_3):
    chip = chip_ref[0]
    for step, out_ref in enumerate((out_0, out_1, out_2, out_3)):
        pair = lax.rem(chip + step, CHIPS) // (CHIPS // 2)
        for group in range(held_ref.shape[0]):
            out_ref[group] = held_ref[group, pair]


def shifted(values, offset):
    amount = (-offset) % POS
    return pltpu.roll(values, amount, values.ndim - 1) if amount else values


def consensus_kernel(
    chip_ref, core_ref, own_0, own_1, own_2, own_3, oth_0, oth_1, oth_2, oth_3, z1_ref, z2_ref, z3_ref,
    keep_ref, give_ref, frame, src, tgt, x1, x2, h2, w3s, kept,
):
    chip = chip_ref[0]
    core = core_ref[0]
    for row in range(HGT):
        frame[row * FRAME : row * FRAME + 8] = jnp.zeros((8, frame.shape[1]), F32)
        frame[row * FRAME + 8 + WID : (row + 1) * FRAME] = jnp.zeros((8, frame.shape[1]), F32)
    for parity, gots in ((core, (own_0, own_1, own_2, own_3)), (1 - core, (oth_0, oth_1, oth_2, oth_3))):
        for step, got in enumerate(gots):
            row = 2 * lax.rem(chip + CHIPS - step, CHIPS) + parity
            for part in range(4):
                to_src = pl.ds(pl.multiple_of(row * FRAME + 8 + part * 8, 8), 8)
                to_tgt = pl.ds(pl.multiple_of(row * WID + part * 8, 8), 8)
                for block in range(8):
                    both = got[part * 8 + block].astype(F32)
                    frame[to_src, block * 128 : block * 128 + 128] = both[:8]
                    tgt[to_tgt, block * 128 : block * 128 + 128] = both[8:]
    for row in range(HGT):
        line = frame[pl.ds(pl.multiple_of(row * FRAME + BLOCK * core, 8), 32), :]
        src[row * 16 : row * 16 + 16] = line[4:20].astype(BF16)
        src[128 + row * 16 : 128 + row * 16 + 16] = line[12:28].astype(BF16)
    corr = lax.dot_general(
        src[...], tgt[...].astype(BF16), (((1,), (1,)), ((), ())), preferred_element_type=F32
    )
    corr = corr.astype(BF16).astype(F32)

    column = lax.broadcasted_iota(jnp.int32, (1, POS), 1)
    line = column // WID
    column = column % WID

    def col_mask(d):
        return ((column + d - 1 >= 0) & (column + d - 1 < WID)).astype(F32)

    def line_mask(c):
        return ((line + c - 1 >= 0) & (line + c - 1 < HGT)).astype(F32)

    has_left = (core > 0).astype(F32)
    has_right = (core < 1).astype(F32)

    z1 = z1_ref[...].astype(F32)
    w1 = [
        jnp.concatenate([pltpu.roll(z1, j + 2 * w, 1) if j + w else z1 for j in range(PART_1)], axis=0).astype(BF16)[:, :K_1]
        for w in range(2)
    ]
    z2 = z2_ref[...].astype(F32)
    rolled = [pltpu.roll(z2, CONV * j, 1) if j else z2 for j in range(PART_2)]
    w2 = jnp.concatenate(
        [rolled[j][c * CONV : c * CONV + CONV] for c in range(3) for j in range(PART_2)], axis=0
    ).astype(BF16)
    z3 = z3_ref[...].astype(F32)
    for j in range(PART_3):
        w3s[:, j, :] = pltpu.roll(z3, CONV * j, 1) if j else z3
    w3 = w3s[...].reshape(27 * PART_3, 256).astype(BF16)[:, :K_3]

    for c in range(3):
        for d in range(3):
            moved = (shifted(corr, WID * (c - 1) + d - 1) * (line_mask(c) * col_mask(d))).astype(BF16)
            for w in range(2):
                at = w * 160
                x1[c * 3 + d, at : at + 16] = jnp.zeros((16, POS), BF16)
                x1[c * 3 + d, at + 16 : at + 144] = moved[w * 128 : w * 128 + 128]
                x1[c * 3 + d, at + 144 : at + 160] = jnp.zeros((16, POS), BF16)
    for d in range(3):
        x2[d, 0:ROWS_1] = jnp.zeros((ROWS_1, POS), BF16)
        x2[d, (HGT + 1) * ROWS_1 :] = jnp.zeros((ROWS_1, POS), BF16)
    left_mask, right_mask = col_mask(0), col_mask(2)
    for i in range(HGT):
        for w in range(2):
            at = w * 160 + 16 * i
            cells = jnp.concatenate([x1[k, at : at + 48] for k in range(9)], axis=0)
            hidden = jnp.maximum(jnp.dot(w1[w], cells, preferred_element_type=F32), 0.0)
            edge = 2 * CONV
            if w == 0:
                hidden = jnp.concatenate([hidden[:edge] * has_left, hidden[edge:]], axis=0)
            else:
                hidden = jnp.concatenate([hidden[: M_1 - edge], hidden[M_1 - edge :] * has_right], axis=0)
            at = (i + 1) * ROWS_1 + w * M_1
            x2[0, at : at + M_1] = (shifted(hidden, -1) * left_mask).astype(BF16)
            x2[1, at : at + M_1] = hidden.astype(BF16)
            x2[2, at : at + M_1] = (shifted(hidden, 1) * right_mask).astype(BF16)

    up_mask, down_mask = line_mask(0), line_mask(2)
    for i in range(HGT):
        for part in range(3):
            first = part * M_2
            cells = jnp.concatenate(
                [x2[d, (i + a) * ROWS_1 + first : (i + a) * ROWS_1 + first + K_PIECE] for d in range(3) for a in range(3)],
                axis=0,
            )
            parts = jnp.dot(w2, cells, preferred_element_type=F32)
            total = parts[M_2 : 2 * M_2]
            total = total + shifted(parts[:M_2], -WID) * up_mask
            total = total + shifted(parts[2 * M_2 :], WID) * down_mask
            total = jnp.maximum(total, 0.0)
            if part == 0:
                total = jnp.concatenate([total[:CONV] * has_left, total[CONV:]], axis=0)
            if part == 2:
                total = jnp.concatenate([total[: M_2 - CONV], total[M_2 - CONV :] * has_right], axis=0)
            h2[i, first : first + M_2] = total.astype(BF16)

    best = None
    sums = [[None] * HGT for _ in range(2)]
    for part in range(2):
        for i in range(HGT):
            parts = jnp.dot(w3, h2[i, part * 128 : part * 128 + K_3], preferred_element_type=F32)
            for a in range(3):
                o = i + 1 - a
                if 0 <= o < HGT:
                    piece = parts[a * 9 * PART_3 : (a + 1) * 9 * PART_3]
                    sums[part][o] = piece if sums[part][o] is None else sums[part][o] + piece
    for i in range(HGT):
        halves = []
        for part in range(2):
            total = None
            for c in range(3):
                for d in range(3):
                    k = (c * 3 + d) * PART_3
                    moved = shifted(sums[part][i][k : k + PART_3], WID * (c - 1) + d - 1) * (line_mask(c) * col_mask(d))
                    total = moved if total is None else total + moved
            halves.append(jnp.maximum(total, 0.0))
        total = jnp.concatenate(halves, axis=0)
        top = jnp.max(total, axis=0, keepdims=True)
        best = top if best is None else jnp.maximum(best, top)
        target_best = jnp.max(total, axis=1, keepdims=True)
        kept[i] = (total * (total / (target_best + EPSILON))).astype(BF16)
    pieces = []
    rest = best
    for _ in range(3):
        piece = rest.astype(BF16).astype(F32)
        pieces.append(piece)
        rest = rest - piece
    pieces = jnp.concatenate(pieces + [jnp.zeros((13, POS), F32)], axis=0).astype(BF16)
    far = CHIPS - 1 - chip
    for ref, parity in ((keep_ref, core), (give_ref, 1 - core)):
        ref[0] = kept[2 * chip + parity]
        ref[1] = kept[2 * far + parity]
        ref[2] = pieces


def finish_kernel(core_ref, keep_ref, got_ref, near_ref, far_ref, lines):
    core = core_ref[0]

    def largest(ref):
        top = ref[2].astype(F32)
        return top[0:1] + top[1:2] + top[2:3]

    best = jnp.maximum(largest(keep_ref), largest(got_ref)) + EPSILON
    for line in range(2):
        lines[line, core] = (keep_ref[line].astype(F32) / best).astype(BF16)
        lines[line, 1 - core] = (got_ref[line].astype(F32) / best).astype(BF16)
    near_ref[...] = lines[0]
    far_ref[...] = lines[1]


def place_kernel(chip_ref, near_ref, far_ref, out_ref):
    pair = chip_ref[0] // (CHIPS // 2)
    for half in range(2):
        out_ref[pair, 0, half * BLOCK : half * BLOCK + BLOCK] = near_ref[half]
        out_ref[1 - pair, 0, half * BLOCK : half * BLOCK + BLOCK] = far_ref[half]


def row_moves(chips, cores):
    return [(2 * y + c, 2 * ((y + chips) % CHIPS) + (c ^ cores)) for y in range(CHIPS) for c in range(2)]


def local(features, src_ids, tgt_ids, image_slot, w_first, w_mid, w_last):
    groups = lax.axis_size("pair")
    channels = features.shape[3]
    place = lax.axis_index("row").astype(jnp.int32)
    chip = (place // 2).reshape(1)
    core = (place % 2).reshape(1)

    taps = w_first.reshape(3, 3, 3, 3, CONV).transpose(4, 2, 3, 0, 1)
    z1 = jnp.pad(taps, ((0, 0),) * 4 + ((1, COLS_IN - 4),)).reshape(CONV, K_1)
    z1 = jnp.pad(z1, ((0, 0), (0, 512 - K_1)))
    taps = w_mid.reshape(3, 3, 3, 3, CONV, CONV).transpose(2, 4, 3, 0, 1, 5)
    z2 = jnp.pad(taps, ((0, 0),) * 4 + ((0, PART_2 - 1), (0, 0))).reshape(3 * CONV, K_2)
    z3 = w_last.reshape(3, 3, 3, 3, CONV).transpose(0, 2, 3, 1, 4).reshape(27, 3 * CONV)
    z3 = jnp.pad(z3, ((0, 0), (0, 256 - 3 * CONV)))

    tiles, slots = call(
        spread_kernel,
        (jax.ShapeDtypeStruct((groups, 16, 128), BF16), jax.ShapeDtypeStruct((2 * src_ids.shape[0],), jnp.int32)),
        (features,),
        (src_ids, tgt_ids, image_slot),
        out_specs=(whole(), whole(pltpu.SMEM)),
    )
    held = lax.all_to_all(tiles, "pair", 0, 0, tiled=True)
    wanted = call(
        select_kernel,
        jax.ShapeDtypeStruct((groups, 2, 16, 128), BF16),
        (held,),
        (slots,),
        (pltpu.VMEM((2 * groups, 8, 128), F32),),
    )
    routed = lax.all_to_all(wanted, "pair", 0, 0, tiled=True)
    sends = call(pack_kernel, (jax.ShapeDtypeStruct((groups, 16, 128), BF16),) * 4, (routed,), (chip,))
    own = [sends[0]] + [lax.ppermute(sends[k], "row", row_moves(k, 0)) for k in range(1, CHIPS)]
    other = [lax.ppermute(block, "row", row_moves(0, 1)) for block in own]
    message = jax.ShapeDtypeStruct((3, 16, POS), BF16)
    keep, give = call(
        consensus_kernel,
        (message, message),
        (*own, *other, z1, z2, z3),
        (chip, core),
        (
            pltpu.VMEM((HGT * FRAME, channels), F32),
            pltpu.VMEM((2 * HGT * COLS_IN, channels), BF16),
            pltpu.VMEM((POS, channels), F32),
            pltpu.VMEM((9, 320, POS), BF16),
            pltpu.VMEM((3, (HGT + 2) * ROWS_1, POS), BF16),
            pltpu.VMEM((HGT, ROWS_2, POS), BF16),
            pltpu.VMEM((27, PART_3, 256), F32),
            pltpu.VMEM((HGT, 16, POS), BF16),
        ),
    )
    got = lax.ppermute(give, "row", row_moves(0, 1))
    lines = jax.ShapeDtypeStruct((2, BLOCK, POS), BF16)
    near, far = call(finish_kernel, (lines, lines), (keep, got), (core,), (pltpu.VMEM((2, 2, BLOCK, POS), BF16),))
    far = lax.ppermute(far, "row", [(2 * y + c, 2 * (CHIPS - 1 - y) + c) for y in range(CHIPS) for c in range(2)])
    return call(place_kernel, jax.ShapeDtypeStruct((2, 1, WID, POS), BF16), (near, far), (chip,))


def solution(mesh):
    placed = (P("pair", "row", None, None), P(), P(), P(), P(), P(), P())
    return jax.shard_map(
        local, mesh=mesh, in_specs=placed, out_specs=P("pair", "row", None, None), check_vma=False
    )
```

```python
import jax
import jax.numpy as jnp
from jax import lax
from jax.experimental import pallas as pl
from jax.experimental.pallas import tpu as pltpu
from jax.sharding import PartitionSpec as P

WID = 32
HGT = 8
POS = HGT * WID
CONV = 16
EPSILON = 1e-05
NORM_EPS = 1e-06
BF16 = jnp.bfloat16
F32 = jnp.float32

CHIPS = 4
BLOCK = WID // 2
COLS_IN = 16
PART_1 = 10
COLS_1, COLS_2 = BLOCK + 4, BLOCK + 2
PART_2 = 6
PART_3 = 8
ROWS_1, ROWS_2 = COLS_1 * CONV, COLS_2 * CONV
K_1 = 27 * COLS_IN
K_PIECE = (PART_2 + 2) * CONV
K_2 = 9 * K_PIECE
M_1 = PART_1 * CONV
M_2 = PART_2 * CONV
K_3 = (PART_3 + 2) * CONV
FRAME = WID + 16


def whole(space=pltpu.VMEM):
    return pl.BlockSpec(memory_space=space)


def call(kernel, out_shape, inputs, scalars=(), scratch=(), out_specs=None):
    return pl.pallas_call(
        kernel,
        out_shape=out_shape,
        in_specs=[whole(pltpu.SMEM)] * len(scalars) + [whole()] * len(inputs),
        out_specs=jax.tree.map(lambda _: whole(), out_shape) if out_specs is None else out_specs,
        scratch_shapes=list(scratch),
        compiler_params=pltpu.CompilerParams(vmem_limit_bytes=48 * 1024 * 1024),
    )(*scalars, *inputs)


def spread_kernel(own_ref, out_ref, rows_ref, sems):
    copies = [
        [
            pltpu.make_async_copy(
                own_ref.at[image, 0, half * 16 : half * 16 + 16], rows_ref.at[image, half], sems.at[image, half]
            )
            for half in range(2)
        ]
        for image in range(2)
    ]
    for half in range(2):
        for image in range(2):
            copies[image][half].start()
    for half in range(2):
        rows = []
        for image in range(2):
            copies[image][half].wait()
            cells = rows_ref[image, half].astype(F32)
            scale = lax.rsqrt(jnp.sum(cells * cells, axis=-1, keepdims=True) + NORM_EPS)
            rows.append(cells * scale)
        for part in range(2):
            for block in range(8):
                at = slice(part * 8, part * 8 + 8), slice(block * 128, block * 128 + 128)
                out_ref[(half * 2 + part) * 8 + block] = jnp.concatenate(
                    [rows[0][at], rows[1][at]], axis=0
                ).astype(BF16)


def slots_kernel(src_ref, tgt_ref, slot_ref, slots_ref):
    for pair in range(src_ref.shape[0]):
        slots_ref[2 * pair] = slot_ref[src_ref[pair]]
        slots_ref[2 * pair + 1] = slot_ref[tgt_ref[pair]]


def select_kernel(slots_ref, held_ref, out_ref, pieces):
    groups = held_ref.shape[0]
    for group in range(groups):
        both = held_ref[group].astype(F32)
        pieces[2 * group] = both[:8]
        pieces[2 * group + 1] = both[8:]
    for group in range(groups):
        for pair in range(2):
            at = 4 * group + 2 * pair
            out_ref[group, pair] = jnp.concatenate(
                [pieces[slots_ref[at]], pieces[slots_ref[at + 1]]], axis=0
            ).astype(BF16)


def pack_kernel(chip_ref, held_ref, out_0, out_1, out_2, out_3):
    chip = chip_ref[0]
    for step, out_ref in enumerate((out_0, out_1, out_2, out_3)):
        pair = lax.rem(chip + step, CHIPS) // (CHIPS // 2)
        for group in range(held_ref.shape[0]):
            out_ref[group] = held_ref[group, pair]


def shifted(values, offset):
    amount = (-offset) % POS
    return pltpu.roll(values, amount, values.ndim - 1) if amount else values


def consensus_kernel(
    chip_ref, core_ref, own_0, own_1, own_2, own_3, oth_0, oth_1, oth_2, oth_3, z1_ref, z2_ref, z3_ref,
    keep_ref, give_ref, frame, src, tgt, x1, x2, h2, w3s, kept,
):
    chip = chip_ref[0]
    core = core_ref[0]
    for row in range(HGT):
        frame[row * FRAME : row * FRAME + 8] = jnp.zeros((8, frame.shape[1]), F32)
        frame[row * FRAME + 8 + WID : (row + 1) * FRAME] = jnp.zeros((8, frame.shape[1]), F32)
    for parity, gots in ((core, (own_0, own_1, own_2, own_3)), (1 - core, (oth_0, oth_1, oth_2, oth_3))):
        for step, got in enumerate(gots):
            row = 2 * lax.rem(chip + CHIPS - step, CHIPS) + parity
            for part in range(4):
                to_src = pl.ds(pl.multiple_of(row * FRAME + 8 + part * 8, 8), 8)
                to_tgt = pl.ds(pl.multiple_of(row * WID + part * 8, 8), 8)
                for block in range(8):
                    both = got[part * 8 + block].astype(F32)
                    frame[to_src, block * 128 : block * 128 + 128] = both[:8]
                    tgt[to_tgt, block * 128 : block * 128 + 128] = both[8:]
    for row in range(HGT):
        line = frame[pl.ds(pl.multiple_of(row * FRAME + BLOCK * core, 8), 32), :]
        src[row * 16 : row * 16 + 16] = line[4:20].astype(BF16)
        src[128 + row * 16 : 128 + row * 16 + 16] = line[12:28].astype(BF16)
    corr = lax.dot_general(
        src[...], tgt[...].astype(BF16), (((1,), (1,)), ((), ())), preferred_element_type=F32
    )
    corr = corr.astype(BF16).astype(F32)

    column = lax.broadcasted_iota(jnp.int32, (1, POS), 1)
    line = column // WID
    column = column % WID

    def col_mask(d):
        return ((column + d - 1 >= 0) & (column + d - 1 < WID)).astype(F32)

    def line_mask(c):
        return ((line + c - 1 >= 0) & (line + c - 1 < HGT)).astype(F32)

    has_left = (core > 0).astype(F32)
    has_right = (core < 1).astype(F32)

    z1 = z1_ref[...].astype(F32)
    w1 = [
        jnp.concatenate([pltpu.roll(z1, j + 2 * w, 1) if j + w else z1 for j in range(PART_1)], axis=0).astype(BF16)[:, :K_1]
        for w in range(2)
    ]
    z2 = z2_ref[...].astype(F32)
    rolled = [pltpu.roll(z2, CONV * j, 1) if j else z2 for j in range(PART_2)]
    w2 = jnp.concatenate(
        [rolled[j][c * CONV : c * CONV + CONV] for c in range(3) for j in range(PART_2)], axis=0
    ).astype(BF16)
    z3 = z3_ref[...].astype(F32)
    for j in range(PART_3):
        w3s[:, j, :] = pltpu.roll(z3, CONV * j, 1) if j else z3
    w3 = w3s[...].reshape(27 * PART_3, 256).astype(BF16)[:, :K_3]

    for c in range(3):
        for d in range(3):
            moved = (shifted(corr, WID * (c - 1) + d - 1) * (line_mask(c) * col_mask(d))).astype(BF16)
            for w in range(2):
                at = w * 160
                x1[c * 3 + d, at : at + 16] = jnp.zeros((16, POS), BF16)
                x1[c * 3 + d, at + 16 : at + 144] = moved[w * 128 : w * 128 + 128]
                x1[c * 3 + d, at + 144 : at + 160] = jnp.zeros((16, POS), BF16)
    for d in range(3):
        x2[d, 0:ROWS_1] = jnp.zeros((ROWS_1, POS), BF16)
        x2[d, (HGT + 1) * ROWS_1 :] = jnp.zeros((ROWS_1, POS), BF16)
    left_mask, right_mask = col_mask(0), col_mask(2)
    for i in range(HGT):
        for w in range(2):
            at = w * 160 + 16 * i
            cells = jnp.concatenate([x1[k, at : at + 48] for k in range(9)], axis=0)
            hidden = jnp.maximum(jnp.dot(w1[w], cells, preferred_element_type=F32), 0.0)
            edge = 2 * CONV
            if w == 0:
                hidden = jnp.concatenate([hidden[:edge] * has_left, hidden[edge:]], axis=0)
            else:
                hidden = jnp.concatenate([hidden[: M_1 - edge], hidden[M_1 - edge :] * has_right], axis=0)
            at = (i + 1) * ROWS_1 + w * M_1
            x2[0, at : at + M_1] = (shifted(hidden, -1) * left_mask).astype(BF16)
            x2[1, at : at + M_1] = hidden.astype(BF16)
            x2[2, at : at + M_1] = (shifted(hidden, 1) * right_mask).astype(BF16)

    up_mask, down_mask = line_mask(0), line_mask(2)
    for i in range(HGT):
        for part in range(3):
            first = part * M_2
            cells = jnp.concatenate(
                [x2[d, (i + a) * ROWS_1 + first : (i + a) * ROWS_1 + first + K_PIECE] for d in range(3) for a in range(3)],
                axis=0,
            )
            parts = jnp.dot(w2, cells, preferred_element_type=F32)
            total = parts[M_2 : 2 * M_2]
            total = total + shifted(parts[:M_2], -WID) * up_mask
            total = total + shifted(parts[2 * M_2 :], WID) * down_mask
            total = jnp.maximum(total, 0.0)
            if part == 0:
                total = jnp.concatenate([total[:CONV] * has_left, total[CONV:]], axis=0)
            if part == 2:
                total = jnp.concatenate([total[: M_2 - CONV], total[M_2 - CONV :] * has_right], axis=0)
            h2[i, first : first + M_2] = total.astype(BF16)

    best = None
    sums = [[None] * HGT for _ in range(2)]
    for part in range(2):
        for i in range(HGT):
            parts = jnp.dot(w3, h2[i, part * 128 : part * 128 + K_3], preferred_element_type=F32)
            for a in range(3):
                o = i + 1 - a
                if 0 <= o < HGT:
                    piece = parts[a * 9 * PART_3 : (a + 1) * 9 * PART_3]
                    sums[part][o] = piece if sums[part][o] is None else sums[part][o] + piece
    for i in range(HGT):
        halves = []
        for part in range(2):
            total = None
            for c in range(3):
                for d in range(3):
                    k = (c * 3 + d) * PART_3
                    moved = shifted(sums[part][i][k : k + PART_3], WID * (c - 1) + d - 1) * (line_mask(c) * col_mask(d))
                    total = moved if total is None else total + moved
            halves.append(jnp.maximum(total, 0.0))
        total = jnp.concatenate(halves, axis=0)
        top = jnp.max(total, axis=0, keepdims=True)
        best = top if best is None else jnp.maximum(best, top)
        target_best = jnp.max(total, axis=1, keepdims=True)
        kept[i] = (total * (total / (target_best + EPSILON))).astype(BF16)
    pieces = []
    rest = best
    for _ in range(3):
        piece = rest.astype(BF16).astype(F32)
        pieces.append(piece)
        rest = rest - piece
    pieces = jnp.concatenate(pieces + [jnp.zeros((13, POS), F32)], axis=0).astype(BF16)
    far = CHIPS - 1 - chip
    for ref, parity in ((keep_ref, core), (give_ref, 1 - core)):
        ref[0] = kept[2 * chip + parity]
        ref[1] = kept[2 * far + parity]
        ref[2] = pieces


def finish_kernel(core_ref, keep_ref, got_ref, near_ref, far_ref, lines):
    core = core_ref[0]

    def largest(ref):
        top = ref[2].astype(F32)
        return top[0:1] + top[1:2] + top[2:3]

    best = jnp.maximum(largest(keep_ref), largest(got_ref)) + EPSILON
    for line in range(2):
        lines[line, core] = (keep_ref[line].astype(F32) / best).astype(BF16)
        lines[line, 1 - core] = (got_ref[line].astype(F32) / best).astype(BF16)
    near_ref[...] = lines[0]
    far_ref[...] = lines[1]


def place_kernel(chip_ref, near_ref, far_ref, out_ref):
    pair = chip_ref[0] // (CHIPS // 2)
    for half in range(2):
        out_ref[pair, 0, half * BLOCK : half * BLOCK + BLOCK] = near_ref[half]
        out_ref[1 - pair, 0, half * BLOCK : half * BLOCK + BLOCK] = far_ref[half]


def row_moves(chips, cores):
    return [(2 * y + c, 2 * ((y + chips) % CHIPS) + (c ^ cores)) for y in range(CHIPS) for c in range(2)]


def local(features, src_ids, tgt_ids, image_slot, w_first, w_mid, w_last):
    groups = lax.axis_size("pair")
    channels = features.shape[3]
    place = lax.axis_index("row").astype(jnp.int32)
    chip = (place // 2).reshape(1)
    core = (place % 2).reshape(1)

    taps = w_first.reshape(3, 3, 3, 3, CONV).transpose(4, 2, 3, 0, 1)
    z1 = jnp.pad(taps, ((0, 0),) * 4 + ((1, COLS_IN - 4),)).reshape(CONV, K_1)
    z1 = jnp.pad(z1, ((0, 0), (0, 512 - K_1)))
    taps = w_mid.reshape(3, 3, 3, 3, CONV, CONV).transpose(2, 4, 3, 0, 1, 5)
    z2 = jnp.pad(taps, ((0, 0),) * 4 + ((0, PART_2 - 1), (0, 0))).reshape(3 * CONV, K_2)
    z3 = w_last.reshape(3, 3, 3, 3, CONV).transpose(0, 2, 3, 1, 4).reshape(27, 3 * CONV)
    z3 = jnp.pad(z3, ((0, 0), (0, 256 - 3 * CONV)))

    tiles = pl.pallas_call(
        spread_kernel,
        out_shape=jax.ShapeDtypeStruct((groups, 16, 128), BF16),
        in_specs=[whole(pl.ANY)],
        out_specs=whole(),
        scratch_shapes=[pltpu.VMEM((2, 2, 16, channels), BF16), pltpu.SemaphoreType.DMA((2, 2))],
    )(features)
    slots = call(
        slots_kernel,
        jax.ShapeDtypeStruct((2 * src_ids.shape[0],), jnp.int32),
        (),
        (src_ids, tgt_ids, image_slot),
        out_specs=whole(pltpu.SMEM),
    )
    held = lax.all_to_all(tiles, "pair", 0, 0, tiled=True)
    wanted = call(
        select_kernel,
        jax.ShapeDtypeStruct((groups, 2, 16, 128), BF16),
        (held,),
        (slots,),
        (pltpu.VMEM((2 * groups, 8, 128), F32),),
    )
    routed = lax.all_to_all(wanted, "pair", 0, 0, tiled=True)
    routed, z1, z2, z3 = lax.optimization_barrier((routed, z1, z2, z3))
    sends = call(pack_kernel, (jax.ShapeDtypeStruct((groups, 16, 128), BF16),) * 4, (routed,), (chip,))
    own = [sends[0]] + [lax.ppermute(sends[k], "row", row_moves(k, 0)) for k in range(1, CHIPS)]
    other = [lax.ppermute(block, "row", row_moves(0, 1)) for block in own]
    message = jax.ShapeDtypeStruct((3, 16, POS), BF16)
    keep, give = call(
        consensus_kernel,
        (message, message),
        (*own, *other, z1, z2, z3),
        (chip, core),
        (
            pltpu.VMEM((HGT * FRAME, channels), F32),
            pltpu.VMEM((2 * HGT * COLS_IN, channels), BF16),
            pltpu.VMEM((POS, channels), F32),
            pltpu.VMEM((9, 320, POS), BF16),
            pltpu.VMEM((3, (HGT + 2) * ROWS_1, POS), BF16),
            pltpu.VMEM((HGT, ROWS_2, POS), BF16),
            pltpu.VMEM((27, PART_3, 256), F32),
            pltpu.VMEM((HGT, 16, POS), BF16),
        ),
    )
    got = lax.ppermute(give, "row", row_moves(0, 1))
    lines = jax.ShapeDtypeStruct((2, BLOCK, POS), BF16)
    near, far = call(finish_kernel, (lines, lines), (keep, got), (core,), (pltpu.VMEM((2, 2, BLOCK, POS), BF16),))
    far = lax.ppermute(far, "row", [(2 * y + c, 2 * (CHIPS - 1 - y) + c) for y in range(CHIPS) for c in range(2)])
    return call(place_kernel, jax.ShapeDtypeStruct((2, 1, WID, POS), BF16), (near, far), (chip,))


def solution(mesh):
    placed = (P("pair", "row", None, None), P(), P(), P(), P(), P(), P())
    return jax.shard_map(
        local, mesh=mesh, in_specs=placed, out_specs=P("pair", "row", None, None), check_vma=False
    )
```

```python
import jax
import jax.numpy as jnp
from jax import lax
from jax.experimental import pallas as pl
from jax.experimental.pallas import tpu as pltpu
from jax.sharding import PartitionSpec as P

WID = 32
HGT = 8
POS = HGT * WID
CONV = 16
EPSILON = 1e-05
NORM_EPS = 1e-06
BF16 = jnp.bfloat16
F32 = jnp.float32

CHIPS = 4
BLOCK = WID // 2
COLS_IN = 16
PART_1 = 10
COLS_1, COLS_2 = BLOCK + 4, BLOCK + 2
PART_2 = 3
PART_3 = 8
ROWS_1, ROWS_2 = COLS_1 * CONV, COLS_2 * CONV
K_1 = 27 * COLS_IN
K_PIECE = (PART_2 + 2) * CONV
K_2 = 3 * K_PIECE
M_1 = PART_1 * CONV
M_2 = PART_2 * CONV
K_3 = (PART_3 + 2) * CONV
FRAME = WID + 16


def whole(space=pltpu.VMEM):
    return pl.BlockSpec(memory_space=space)


def call(kernel, out_shape, inputs, scalars=(), scratch=(), out_specs=None):
    return pl.pallas_call(
        kernel,
        out_shape=out_shape,
        in_specs=[whole(pltpu.SMEM)] * len(scalars) + [whole()] * len(inputs),
        out_specs=jax.tree.map(lambda _: whole(), out_shape) if out_specs is None else out_specs,
        scratch_shapes=list(scratch),
        compiler_params=pltpu.CompilerParams(vmem_limit_bytes=48 * 1024 * 1024),
    )(*scalars, *inputs)


def spread_kernel(own_ref, out_ref):
    rows = []
    for image in range(2):
        cells = own_ref[image, 0].astype(F32)
        scale = lax.rsqrt(jnp.sum(cells * cells, axis=-1, keepdims=True) + NORM_EPS)
        rows.append(cells * scale)
    for part in range(4):
        for block in range(8):
            at = slice(part * 8, part * 8 + 8), slice(block * 128, block * 128 + 128)
            out_ref[part * 8 + block] = jnp.concatenate([rows[0][at], rows[1][at]], axis=0).astype(BF16)


def slots_kernel(src_ref, tgt_ref, slot_ref, slots_ref):
    for pair in range(src_ref.shape[0]):
        slots_ref[2 * pair] = slot_ref[src_ref[pair]]
        slots_ref[2 * pair + 1] = slot_ref[tgt_ref[pair]]


def select_kernel(slots_ref, held_ref, out_ref, pieces):
    groups = held_ref.shape[0]
    for group in range(groups):
        both = held_ref[group].astype(F32)
        pieces[2 * group] = both[:8]
        pieces[2 * group + 1] = both[8:]
    for group in range(groups):
        for pair in range(2):
            at = 4 * group + 2 * pair
            out_ref[group, pair] = jnp.concatenate(
                [pieces[slots_ref[at]], pieces[slots_ref[at + 1]]], axis=0
            ).astype(BF16)


def pack_kernel(chip_ref, held_ref, out_0, out_1, out_2, out_3):
    chip = chip_ref[0]
    for step, out_ref in enumerate((out_0, out_1, out_2, out_3)):
        pair = lax.rem(chip + step, CHIPS) // (CHIPS // 2)
        for group in range(held_ref.shape[0]):
            out_ref[group] = held_ref[group, pair]


def shifted(values, offset):
    amount = (-offset) % POS
    return pltpu.roll(values, amount, values.ndim - 1) if amount else values


def consensus_kernel(
    chip_ref, core_ref, own_0, own_1, own_2, own_3, oth_0, oth_1, oth_2, oth_3, z1_ref, z2_ref, z3_ref,
    keep_ref, give_ref, frame, src, tgt, x1, x2, h2, w3s, kept,
):
    chip = chip_ref[0]
    core = core_ref[0]
    for row in range(HGT):
        frame[row * FRAME : row * FRAME + 8] = jnp.zeros((8, frame.shape[1]), F32)
        frame[row * FRAME + 8 + WID : (row + 1) * FRAME] = jnp.zeros((8, frame.shape[1]), F32)
    for parity, gots in ((core, (own_0, own_1, own_2, own_3)), (1 - core, (oth_0, oth_1, oth_2, oth_3))):
        for step, got in enumerate(gots):
            row = 2 * lax.rem(chip + CHIPS - step, CHIPS) + parity
            for part in range(4):
                to_src = pl.ds(pl.multiple_of(row * FRAME + 8 + part * 8, 8), 8)
                to_tgt = pl.ds(pl.multiple_of(row * WID + part * 8, 8), 8)
                for block in range(8):
                    both = got[part * 8 + block].astype(F32)
                    frame[to_src, block * 128 : block * 128 + 128] = both[:8]
                    tgt[to_tgt, block * 128 : block * 128 + 128] = both[8:]
    for row in range(HGT):
        line = frame[pl.ds(pl.multiple_of(row * FRAME + BLOCK * core, 8), 32), :]
        src[row * 16 : row * 16 + 16] = line[4:20].astype(BF16)
        src[128 + row * 16 : 128 + row * 16 + 16] = line[12:28].astype(BF16)
    corr = lax.dot_general(
        src[...], tgt[...].astype(BF16), (((1,), (1,)), ((), ())), preferred_element_type=F32
    )
    corr = corr.astype(BF16).astype(F32)

    column = lax.broadcasted_iota(jnp.int32, (1, POS), 1)
    line = column // WID
    column = column % WID

    def col_mask(d):
        return ((column + d - 1 >= 0) & (column + d - 1 < WID)).astype(F32)

    def line_mask(c):
        return ((line + c - 1 >= 0) & (line + c - 1 < HGT)).astype(F32)

    has_left = (core > 0).astype(F32)
    has_right = (core < 1).astype(F32)

    z1 = z1_ref[...].astype(F32)
    w1 = [
        jnp.concatenate([pltpu.roll(z1, j + 2 * w, 1) if j + w else z1 for j in range(PART_1)], axis=0).astype(BF16)[:, :K_1]
        for w in range(2)
    ]
    z2 = z2_ref[...].astype(F32)
    rolled = [pltpu.roll(z2, CONV * j, 1) if j else z2 for j in range(PART_2)]
    w2 = jnp.concatenate(
        [rolled[j][k * CONV : k * CONV + CONV] for k in range(9) for j in range(PART_2)], axis=0
    ).astype(BF16)[:, :K_2]
    z3 = z3_ref[...].astype(F32)
    for j in range(PART_3):
        w3s[:, j, :] = pltpu.roll(z3, CONV * j, 1) if j else z3
    w3 = w3s[...].reshape(27 * PART_3, 256).astype(BF16)[:, :K_3]

    for c in range(3):
        for d in range(3):
            moved = (shifted(corr, WID * (c - 1) + d - 1) * (line_mask(c) * col_mask(d))).astype(BF16)
            for w in range(2):
                at = w * 160
                x1[c * 3 + d, at : at + 16] = jnp.zeros((16, POS), BF16)
                x1[c * 3 + d, at + 16 : at + 144] = moved[w * 128 : w * 128 + 128]
                x1[c * 3 + d, at + 144 : at + 160] = jnp.zeros((16, POS), BF16)
    left_mask, right_mask = col_mask(0), col_mask(2)
    for i in range(HGT):
        for w in range(2):
            at = w * 160 + 16 * i
            cells = jnp.concatenate([x1[k, at : at + 48] for k in range(9)], axis=0)
            hidden = jnp.maximum(jnp.dot(w1[w], cells, preferred_element_type=F32), 0.0)
            edge = 2 * CONV
            if w == 0:
                hidden = jnp.concatenate([hidden[:edge] * has_left, hidden[edge:]], axis=0)
            else:
                hidden = jnp.concatenate([hidden[: M_1 - edge], hidden[M_1 - edge :] * has_right], axis=0)
            at = i * ROWS_1 + w * M_1
            x2[0, at : at + M_1] = (shifted(hidden, -1) * left_mask).astype(BF16)
            x2[1, at : at + M_1] = hidden.astype(BF16)
            x2[2, at : at + M_1] = (shifted(hidden, 1) * right_mask).astype(BF16)

    up_mask, down_mask = line_mask(0), line_mask(2)
    for part in range(COLS_2 // PART_2):
        first = part * M_2
        rows = [None] * HGT
        for i in range(HGT):
            cells = jnp.concatenate([x2[d, i * ROWS_1 + first : i * ROWS_1 + first + K_PIECE] for d in range(3)], axis=0)
            low, high = (0 if i < HGT - 1 else 1), (3 if i > 0 else 2)
            parts = jnp.dot(w2[low * 3 * M_2 : high * 3 * M_2], cells, preferred_element_type=F32)
            for a in range(low, high):
                piece = parts[(a - low) * 3 * M_2 : (a - low + 1) * 3 * M_2]
                o = i + 1 - a
                rows[o] = piece if rows[o] is None else rows[o] + piece
            done = [i - 1] if i < HGT - 1 else [i - 1, i]
            for o in done:
                if o < 0:
                    continue
                total = rows[o][M_2 : 2 * M_2]
                total = total + shifted(rows[o][:M_2], -WID) * up_mask
                total = total + shifted(rows[o][2 * M_2 :], WID) * down_mask
                total = jnp.maximum(total, 0.0)
                if part == 0:
                    total = jnp.concatenate([total[:CONV] * has_left, total[CONV:]], axis=0)
                if part == COLS_2 // PART_2 - 1:
                    total = jnp.concatenate([total[: M_2 - CONV], total[M_2 - CONV :] * has_right], axis=0)
                h2[o, first : first + M_2] = total.astype(BF16)

    best = None
    sums = [[None] * HGT for _ in range(2)]
    for part in range(2):
        for i in range(HGT):
            parts = jnp.dot(w3, h2[i, part * 128 : part * 128 + K_3], preferred_element_type=F32)
            for a in range(3):
                o = i + 1 - a
                if 0 <= o < HGT:
                    piece = parts[a * 9 * PART_3 : (a + 1) * 9 * PART_3]
                    sums[part][o] = piece if sums[part][o] is None else sums[part][o] + piece
    for i in range(HGT):
        halves = []
        for part in range(2):
            total = None
            for c in range(3):
                for d in range(3):
                    k = (c * 3 + d) * PART_3
                    moved = shifted(sums[part][i][k : k + PART_3], WID * (c - 1) + d - 1) * (line_mask(c) * col_mask(d))
                    total = moved if total is None else total + moved
            halves.append(jnp.maximum(total, 0.0))
        total = jnp.concatenate(halves, axis=0)
        top = jnp.max(total, axis=0, keepdims=True)
        best = top if best is None else jnp.maximum(best, top)
        target_best = jnp.max(total, axis=1, keepdims=True)
        kept[i] = (total * (total / (target_best + EPSILON))).astype(BF16)
    pieces = []
    rest = best
    for _ in range(3):
        piece = rest.astype(BF16).astype(F32)
        pieces.append(piece)
        rest = rest - piece
    pieces = jnp.concatenate(pieces + [jnp.zeros((13, POS), F32)], axis=0).astype(BF16)
    far = CHIPS - 1 - chip
    for ref, parity in ((keep_ref, core), (give_ref, 1 - core)):
        ref[0] = kept[2 * chip + parity]
        ref[1] = kept[2 * far + parity]
        ref[2] = pieces


def consensus_scratch(channels):
    return (
        pltpu.VMEM((HGT * FRAME, channels), F32),
        pltpu.VMEM((2 * HGT * COLS_IN, channels), BF16),
        pltpu.VMEM((POS, channels), F32),
        pltpu.VMEM((9, 320, POS), BF16),
        pltpu.VMEM((3, HGT * ROWS_1, POS), BF16),
        pltpu.VMEM((HGT, ROWS_2, POS), BF16),
        pltpu.VMEM((27, PART_3, 256), F32),
        pltpu.VMEM((HGT, 16, POS), BF16),
    )


def finish_kernel(core_ref, keep_ref, got_ref, near_ref, far_ref, lines):
    core = core_ref[0]

    def largest(ref):
        top = ref[2].astype(F32)
        return top[0:1] + top[1:2] + top[2:3]

    best = jnp.maximum(largest(keep_ref), largest(got_ref)) + EPSILON
    for line in range(2):
        lines[line, core] = (keep_ref[line].astype(F32) / best).astype(BF16)
        lines[line, 1 - core] = (got_ref[line].astype(F32) / best).astype(BF16)
    near_ref[...] = lines[0]
    far_ref[...] = lines[1]


def place_kernel(chip_ref, near_ref, far_ref, out_ref):
    pair = chip_ref[0] // (CHIPS // 2)
    for half in range(2):
        out_ref[pair, 0, half * BLOCK : half * BLOCK + BLOCK] = near_ref[half]
        out_ref[1 - pair, 0, half * BLOCK : half * BLOCK + BLOCK] = far_ref[half]


def row_moves(chips, cores):
    return [(2 * y + c, 2 * ((y + chips) % CHIPS) + (c ^ cores)) for y in range(CHIPS) for c in range(2)]


def local(features, src_ids, tgt_ids, image_slot, w_first, w_mid, w_last):
    groups = lax.axis_size("pair")
    channels = features.shape[3]
    place = lax.axis_index("row").astype(jnp.int32)
    chip = (place // 2).reshape(1)
    core = (place % 2).reshape(1)

    taps = w_first.reshape(3, 3, 3, 3, CONV).transpose(4, 2, 3, 0, 1)
    z1 = jnp.pad(taps, ((0, 0),) * 4 + ((1, COLS_IN - 4),)).reshape(CONV, K_1)
    z1 = jnp.pad(z1, ((0, 0), (0, 512 - K_1)))
    taps = w_mid.reshape(3, 3, 3, 3, CONV, CONV).transpose(0, 2, 4, 3, 1, 5)
    z2 = jnp.pad(taps, ((0, 0),) * 4 + ((0, PART_2 - 1), (0, 0))).reshape(9 * CONV, K_2)
    z2 = jnp.pad(z2, ((0, 0), (0, 256 - K_2)))
    z3 = w_last.reshape(3, 3, 3, 3, CONV).transpose(0, 2, 3, 1, 4).reshape(27, 3 * CONV)
    z3 = jnp.pad(z3, ((0, 0), (0, 256 - 3 * CONV)))

    tiles = call(spread_kernel, jax.ShapeDtypeStruct((groups, 16, 128), BF16), (features,))
    slots = call(
        slots_kernel,
        jax.ShapeDtypeStruct((2 * src_ids.shape[0],), jnp.int32),
        (),
        (src_ids, tgt_ids, image_slot),
        out_specs=whole(pltpu.SMEM),
    )
    held = lax.all_to_all(tiles, "pair", 0, 0, tiled=True)
    wanted = call(
        select_kernel,
        jax.ShapeDtypeStruct((groups, 2, 16, 128), BF16),
        (held,),
        (slots,),
        (pltpu.VMEM((2 * groups, 8, 128), F32),),
    )
    routed = lax.all_to_all(wanted, "pair", 0, 0, tiled=True)
    routed, z1, z2, z3 = lax.optimization_barrier((routed, z1, z2, z3))
    sends = call(pack_kernel, (jax.ShapeDtypeStruct((groups, 16, 128), BF16),) * 4, (routed,), (chip,))
    own = [sends[0]] + [lax.ppermute(sends[k], "row", row_moves(k, 0)) for k in range(1, CHIPS)]
    other = [lax.ppermute(block, "row", row_moves(0, 1)) for block in own]
    message = jax.ShapeDtypeStruct((3, 16, POS), BF16)
    keep, give = call(
        consensus_kernel,
        (message, message),
        (*own, *other, z1, z2, z3),
        (chip, core),
        consensus_scratch(channels),
    )
    got = lax.ppermute(give, "row", row_moves(0, 1))
    lines = jax.ShapeDtypeStruct((2, BLOCK, POS), BF16)
    near, far = call(finish_kernel, (lines, lines), (keep, got), (core,), (pltpu.VMEM((2, 2, BLOCK, POS), BF16),))
    far = lax.ppermute(far, "row", [(2 * y + c, 2 * (CHIPS - 1 - y) + c) for y in range(CHIPS) for c in range(2)])
    return call(place_kernel, jax.ShapeDtypeStruct((2, 1, WID, POS), BF16), (near, far), (chip,))


def solution(mesh):
    placed = (P("pair", "row", None, None), P(), P(), P(), P(), P(), P())
    return jax.shard_map(
        local, mesh=mesh, in_specs=placed, out_specs=P("pair", "row", None, None), check_vma=False
    )
```

```python
import jax
import jax.numpy as jnp
from jax import lax
from jax.experimental import pallas as pl
from jax.experimental.pallas import tpu as pltpu
from jax.sharding import PartitionSpec as P

WID = 32
HGT = 8
POS = HGT * WID
CONV = 16
EPSILON = 1e-05
NORM_EPS = 1e-06
BF16 = jnp.bfloat16
F32 = jnp.float32

CHIPS = 4
BLOCK = WID // 2
COLS_IN = 16
PART_1 = 10
COLS_1, COLS_2 = BLOCK + 4, BLOCK + 2
PART_2 = 3
PART_3 = 8
ROWS_1, ROWS_2 = COLS_1 * CONV, COLS_2 * CONV
K_1 = 27 * COLS_IN
K_PIECE = (PART_2 + 2) * CONV
K_2 = 3 * K_PIECE
M_1 = PART_1 * CONV
M_2 = PART_2 * CONV
K_3 = (PART_3 + 2) * CONV
FRAME = WID + 16


def whole(space=pltpu.VMEM):
    return pl.BlockSpec(memory_space=space)


def call(kernel, out_shape, inputs, scalars=(), scratch=(), out_specs=None):
    return pl.pallas_call(
        kernel,
        out_shape=out_shape,
        in_specs=[whole(pltpu.SMEM)] * len(scalars) + [whole()] * len(inputs),
        out_specs=jax.tree.map(lambda _: whole(), out_shape) if out_specs is None else out_specs,
        scratch_shapes=list(scratch),
        compiler_params=pltpu.CompilerParams(vmem_limit_bytes=48 * 1024 * 1024),
    )(*scalars, *inputs)


def spread_kernel(src_hbm, tgt_hbm, slot_hbm, own_hbm, out_ref, slots_ref, src_ref, tgt_ref, slot_ref, rows_ref, sems):
    loads = [
        pltpu.make_async_copy(hbm, ref, sems.at[place])
        for place, (hbm, ref) in enumerate(((src_hbm, src_ref), (tgt_hbm, tgt_ref), (slot_hbm, slot_ref)))
    ]
    for load in loads:
        load.start()
    rows_load = pltpu.make_async_copy(own_hbm, rows_ref, sems.at[3])
    rows_load.start()
    for load in loads:
        load.wait()
    batch = 16
    for first in range(0, src_ref.shape[0], batch):
        pairs = range(first, first + batch)
        ids = [ref[pair] for pair in pairs for ref in (src_ref, tgt_ref)]
        for place, slot in enumerate([slot_ref[image] for image in ids]):
            slots_ref[2 * first + place] = slot
    rows_load.wait()
    rows = []
    for image in range(2):
        cells = rows_ref[image, 0].astype(F32)
        scale = lax.rsqrt(jnp.sum(cells * cells, axis=-1, keepdims=True) + NORM_EPS)
        rows.append(cells * scale)
    for part in range(4):
        for block in range(8):
            at = slice(part * 8, part * 8 + 8), slice(block * 128, block * 128 + 128)
            out_ref[part * 8 + block] = jnp.concatenate([rows[0][at], rows[1][at]], axis=0).astype(BF16)


def select_kernel(slots_ref, held_ref, out_ref, pieces):
    groups = held_ref.shape[0]
    for group in range(groups):
        both = held_ref[group].astype(F32)
        pieces[2 * group] = both[:8]
        pieces[2 * group + 1] = both[8:]
    batch = 4
    for first in range(0, groups, batch):
        slots = [slots_ref[4 * first + place] for place in range(4 * batch)]
        found = [pieces[slot] for slot in slots]
        for at in range(2 * batch):
            both = jnp.concatenate([found[2 * at], found[2 * at + 1]], axis=0)
            out_ref[first + at // 2, at % 2] = both.astype(BF16)


def pack_kernel(chip_ref, held_ref, out_0, out_1, out_2, out_3):
    chip = chip_ref[0]
    for step, out_ref in enumerate((out_0, out_1, out_2, out_3)):
        pair = lax.rem(chip + step, CHIPS) // (CHIPS // 2)
        for group in range(held_ref.shape[0]):
            out_ref[group] = held_ref[group, pair]


def shifted(values, offset):
    amount = (-offset) % POS
    return pltpu.roll(values, amount, values.ndim - 1) if amount else values


def consensus_kernel(
    chip_ref, core_ref, own_0, own_1, own_2, own_3, oth_0, oth_1, oth_2, oth_3, z1_ref, z2_ref, z3_ref,
    keep_ref, give_ref, frame, src, tgt, x1, x2, h2, w3s, kept,
):
    chip = chip_ref[0]
    core = core_ref[0]
    for row in range(HGT):
        frame[row * FRAME : row * FRAME + 8] = jnp.zeros((8, frame.shape[1]), F32)
        frame[row * FRAME + 8 + WID : (row + 1) * FRAME] = jnp.zeros((8, frame.shape[1]), F32)
    for parity, gots in ((core, (own_0, own_1, own_2, own_3)), (1 - core, (oth_0, oth_1, oth_2, oth_3))):
        for step, got in enumerate(gots):
            row = 2 * lax.rem(chip + CHIPS - step, CHIPS) + parity
            for part in range(4):
                to_src = pl.ds(pl.multiple_of(row * FRAME + 8 + part * 8, 8), 8)
                to_tgt = pl.ds(pl.multiple_of(row * WID + part * 8, 8), 8)
                for block in range(8):
                    both = got[part * 8 + block].astype(F32)
                    frame[to_src, block * 128 : block * 128 + 128] = both[:8]
                    tgt[to_tgt, block * 128 : block * 128 + 128] = both[8:]
    for row in range(HGT):
        line = frame[pl.ds(pl.multiple_of(row * FRAME + BLOCK * core, 8), 32), :]
        src[row * 16 : row * 16 + 16] = line[4:20].astype(BF16)
        src[128 + row * 16 : 128 + row * 16 + 16] = line[12:28].astype(BF16)
    corr = lax.dot_general(
        src[...], tgt[...].astype(BF16), (((1,), (1,)), ((), ())), preferred_element_type=F32
    )
    corr = corr.astype(BF16).astype(F32)

    column = lax.broadcasted_iota(jnp.int32, (1, POS), 1)
    line = column // WID
    column = column % WID

    def col_mask(d):
        return ((column + d - 1 >= 0) & (column + d - 1 < WID)).astype(F32)

    def line_mask(c):
        return ((line + c - 1 >= 0) & (line + c - 1 < HGT)).astype(F32)

    has_left = (core > 0).astype(F32)
    has_right = (core < 1).astype(F32)

    z1 = z1_ref[...].astype(F32)
    w1 = [
        jnp.concatenate([pltpu.roll(z1, j + 2 * w, 1) if j + w else z1 for j in range(PART_1)], axis=0).astype(BF16)[:, :K_1]
        for w in range(2)
    ]
    z2 = z2_ref[...].astype(F32)
    rolled = [pltpu.roll(z2, CONV * j, 1) if j else z2 for j in range(PART_2)]
    w2 = jnp.concatenate(
        [rolled[j][k * CONV : k * CONV + CONV] for k in range(9) for j in range(PART_2)], axis=0
    ).astype(BF16)[:, :K_2]
    z3 = z3_ref[...].astype(F32)
    for j in range(PART_3):
        w3s[:, j, :] = pltpu.roll(z3, CONV * j, 1) if j else z3
    w3 = w3s[...].reshape(27 * PART_3, 256).astype(BF16)[:, :K_3]

    for c in range(3):
        for d in range(3):
            moved = (shifted(corr, WID * (c - 1) + d - 1) * (line_mask(c) * col_mask(d))).astype(BF16)
            for w in range(2):
                at = w * 160
                x1[c * 3 + d, at : at + 16] = jnp.zeros((16, POS), BF16)
                x1[c * 3 + d, at + 16 : at + 144] = moved[w * 128 : w * 128 + 128]
                x1[c * 3 + d, at + 144 : at + 160] = jnp.zeros((16, POS), BF16)
    left_mask, right_mask = col_mask(0), col_mask(2)
    for i in range(HGT):
        for w in range(2):
            at = w * 160 + 16 * i
            cells = jnp.concatenate([x1[k, at : at + 48] for k in range(9)], axis=0)
            hidden = jnp.maximum(jnp.dot(w1[w], cells, preferred_element_type=F32), 0.0)
            edge = 2 * CONV
            if w == 0:
                hidden = jnp.concatenate([hidden[:edge] * has_left, hidden[edge:]], axis=0)
            else:
                hidden = jnp.concatenate([hidden[: M_1 - edge], hidden[M_1 - edge :] * has_right], axis=0)
            at = i * ROWS_1 + w * M_1
            x2[0, at : at + M_1] = (shifted(hidden, -1) * left_mask).astype(BF16)
            x2[1, at : at + M_1] = hidden.astype(BF16)
            x2[2, at : at + M_1] = (shifted(hidden, 1) * right_mask).astype(BF16)

    up_mask, down_mask = line_mask(0), line_mask(2)
    for part in range(COLS_2 // PART_2):
        first = part * M_2
        rows = [None] * HGT
        for i in range(HGT):
            cells = jnp.concatenate([x2[d, i * ROWS_1 + first : i * ROWS_1 + first + K_PIECE] for d in range(3)], axis=0)
            low, high = (0 if i < HGT - 1 else 1), (3 if i > 0 else 2)
            parts = jnp.dot(w2[low * 3 * M_2 : high * 3 * M_2], cells, preferred_element_type=F32)
            for a in range(low, high):
                piece = parts[(a - low) * 3 * M_2 : (a - low + 1) * 3 * M_2]
                o = i + 1 - a
                rows[o] = piece if rows[o] is None else rows[o] + piece
            done = [i - 1] if i < HGT - 1 else [i - 1, i]
            for o in done:
                if o < 0:
                    continue
                total = rows[o][M_2 : 2 * M_2]
                total = total + shifted(rows[o][:M_2], -WID) * up_mask
                total = total + shifted(rows[o][2 * M_2 :], WID) * down_mask
                total = jnp.maximum(total, 0.0)
                if part == 0:
                    total = jnp.concatenate([total[:CONV] * has_left, total[CONV:]], axis=0)
                if part == COLS_2 // PART_2 - 1:
                    total = jnp.concatenate([total[: M_2 - CONV], total[M_2 - CONV :] * has_right], axis=0)
                h2[o, first : first + M_2] = total.astype(BF16)

    best = None
    sums = [[None] * HGT for _ in range(2)]
    for part in range(2):
        for i in range(HGT):
            parts = jnp.dot(w3, h2[i, part * 128 : part * 128 + K_3], preferred_element_type=F32)
            for a in range(3):
                o = i + 1 - a
                if 0 <= o < HGT:
                    piece = parts[a * 9 * PART_3 : (a + 1) * 9 * PART_3]
                    sums[part][o] = piece if sums[part][o] is None else sums[part][o] + piece
    for i in range(HGT):
        halves = []
        for part in range(2):
            total = None
            for c in range(3):
                for d in range(3):
                    k = (c * 3 + d) * PART_3
                    moved = shifted(sums[part][i][k : k + PART_3], WID * (c - 1) + d - 1) * (line_mask(c) * col_mask(d))
                    total = moved if total is None else total + moved
            halves.append(jnp.maximum(total, 0.0))
        total = jnp.concatenate(halves, axis=0)
        top = jnp.max(total, axis=0, keepdims=True)
        best = top if best is None else jnp.maximum(best, top)
        target_best = jnp.max(total, axis=1, keepdims=True)
        kept[i] = (total * (total / (target_best + EPSILON))).astype(BF16)
    pieces = []
    rest = best
    for _ in range(3):
        piece = rest.astype(BF16).astype(F32)
        pieces.append(piece)
        rest = rest - piece
    pieces = jnp.concatenate(pieces + [jnp.zeros((13, POS), F32)], axis=0).astype(BF16)
    far = CHIPS - 1 - chip
    for ref, parity in ((keep_ref, core), (give_ref, 1 - core)):
        ref[0] = kept[2 * chip + parity]
        ref[1] = kept[2 * far + parity]
        ref[2] = pieces


def consensus_scratch(channels):
    return (
        pltpu.VMEM((HGT * FRAME, channels), F32),
        pltpu.VMEM((2 * HGT * COLS_IN, channels), BF16),
        pltpu.VMEM((POS, channels), F32),
        pltpu.VMEM((9, 320, POS), BF16),
        pltpu.VMEM((3, HGT * ROWS_1, POS), BF16),
        pltpu.VMEM((HGT, ROWS_2, POS), BF16),
        pltpu.VMEM((27, PART_3, 256), F32),
        pltpu.VMEM((HGT, 16, POS), BF16),
    )


def finish_kernel(core_ref, keep_ref, got_ref, near_ref, far_ref, lines):
    core = core_ref[0]

    def largest(ref):
        top = ref[2].astype(F32)
        return top[0:1] + top[1:2] + top[2:3]

    best = jnp.maximum(largest(keep_ref), largest(got_ref)) + EPSILON
    for line in range(2):
        lines[line, core] = (keep_ref[line].astype(F32) / best).astype(BF16)
        lines[line, 1 - core] = (got_ref[line].astype(F32) / best).astype(BF16)
    near_ref[...] = lines[0]
    far_ref[...] = lines[1]


def place_kernel(chip_ref, near_ref, far_ref, out_ref):
    pair = chip_ref[0] // (CHIPS // 2)
    for half in range(2):
        out_ref[pair, 0, half * BLOCK : half * BLOCK + BLOCK] = near_ref[half]
        out_ref[1 - pair, 0, half * BLOCK : half * BLOCK + BLOCK] = far_ref[half]


def row_moves(chips, cores):
    return [(2 * y + c, 2 * ((y + chips) % CHIPS) + (c ^ cores)) for y in range(CHIPS) for c in range(2)]


def local(features, src_ids, tgt_ids, image_slot, w_first, w_mid, w_last):
    groups = lax.axis_size("pair")
    channels = features.shape[3]
    place = lax.axis_index("row").astype(jnp.int32)
    chip = (place // 2).reshape(1)
    core = (place % 2).reshape(1)

    ids = src_ids.shape
    tiles, slots = pl.pallas_call(
        spread_kernel,
        out_shape=(jax.ShapeDtypeStruct((groups, 16, 128), BF16), jax.ShapeDtypeStruct((2 * ids[0],), jnp.int32)),
        in_specs=[whole(pl.ANY)] * 4,
        out_specs=(whole(), whole(pltpu.SMEM)),
        scratch_shapes=[
            pltpu.SMEM(ids, jnp.int32),
            pltpu.SMEM(ids, jnp.int32),
            pltpu.SMEM(image_slot.shape, jnp.int32),
            pltpu.VMEM(features.shape, BF16),
            pltpu.SemaphoreType.DMA((4,)),
        ],
    )(src_ids, tgt_ids, image_slot, features)
    held = lax.all_to_all(tiles, "pair", 0, 0, tiled=True)
    held, w_first, w_mid, w_last = lax.optimization_barrier((held, w_first, w_mid, w_last))
    wanted = call(
        select_kernel,
        jax.ShapeDtypeStruct((groups, 2, 16, 128), BF16),
        (held,),
        (slots,),
        (pltpu.VMEM((2 * groups, 8, 128), F32),),
    )
    routed = lax.all_to_all(wanted, "pair", 0, 0, tiled=True)
    taps = w_first.reshape(3, 3, 3, 3, CONV).transpose(4, 2, 3, 0, 1)
    z1 = jnp.pad(taps, ((0, 0),) * 4 + ((1, COLS_IN - 4),)).reshape(CONV, K_1)
    z1 = jnp.pad(z1, ((0, 0), (0, 512 - K_1)))
    taps = w_mid.reshape(3, 3, 3, 3, CONV, CONV).transpose(0, 2, 4, 3, 1, 5)
    z2 = jnp.pad(taps, ((0, 0),) * 4 + ((0, PART_2 - 1), (0, 0))).reshape(9 * CONV, K_2)
    z2 = jnp.pad(z2, ((0, 0), (0, 256 - K_2)))
    z3 = w_last.reshape(3, 3, 3, 3, CONV).transpose(0, 2, 3, 1, 4).reshape(27, 3 * CONV)
    z3 = jnp.pad(z3, ((0, 0), (0, 256 - 3 * CONV)))

    routed, z1, z2, z3 = lax.optimization_barrier((routed, z1, z2, z3))
    sends = call(pack_kernel, (jax.ShapeDtypeStruct((groups, 16, 128), BF16),) * 4, (routed,), (chip,))
    own = [sends[0]] + [lax.ppermute(sends[k], "row", row_moves(k, 0)) for k in range(1, CHIPS)]
    other = [lax.ppermute(block, "row", row_moves(0, 1)) for block in own]
    message = jax.ShapeDtypeStruct((3, 16, POS), BF16)
    keep, give = call(
        consensus_kernel,
        (message, message),
        (*own, *other, z1, z2, z3),
        (chip, core),
        consensus_scratch(channels),
    )
    got = lax.ppermute(give, "row", row_moves(0, 1))
    lines = jax.ShapeDtypeStruct((2, BLOCK, POS), BF16)
    near, far = call(finish_kernel, (lines, lines), (keep, got), (core,), (pltpu.VMEM((2, 2, BLOCK, POS), BF16),))
    far = lax.ppermute(far, "row", [(2 * y + c, 2 * (CHIPS - 1 - y) + c) for y in range(CHIPS) for c in range(2)])
    return call(place_kernel, jax.ShapeDtypeStruct((2, 1, WID, POS), BF16), (near, far), (chip,))


def solution(mesh):
    placed = (P("pair", "row", None, None), P(), P(), P(), P(), P(), P())
    return jax.shard_map(
        local, mesh=mesh, in_specs=placed, out_specs=P("pair", "row", None, None), check_vma=False
    )
```

```python
import jax
import jax.numpy as jnp
from jax import lax
from jax.experimental import pallas as pl
from jax.experimental.pallas import tpu as pltpu
from jax.sharding import PartitionSpec as P

WID = 32
HGT = 8
POS = HGT * WID
CONV = 16
EPSILON = 1e-05
NORM_EPS = 1e-06
BF16 = jnp.bfloat16
F32 = jnp.float32

CHIPS = 4
BLOCK = WID // 2
COLS_IN = 16
PART_1 = 10
COLS_1, COLS_2 = BLOCK + 4, BLOCK + 2
PART_2 = 3
PART_3 = 8
ROWS_1, ROWS_2 = COLS_1 * CONV, COLS_2 * CONV
K_1 = 27 * COLS_IN
K_PIECE = (PART_2 + 2) * CONV
K_2 = 3 * K_PIECE
M_1 = PART_1 * CONV
M_2 = PART_2 * CONV
K_3 = (PART_3 + 2) * CONV
FRAME = WID + 16


def whole(space=pltpu.VMEM):
    return pl.BlockSpec(memory_space=space)


def call(kernel, out_shape, inputs, scalars=(), scratch=(), out_specs=None):
    return pl.pallas_call(
        kernel,
        out_shape=out_shape,
        in_specs=[whole(pltpu.SMEM)] * len(scalars) + [whole()] * len(inputs),
        out_specs=jax.tree.map(lambda _: whole(), out_shape) if out_specs is None else out_specs,
        scratch_shapes=list(scratch),
        compiler_params=pltpu.CompilerParams(vmem_limit_bytes=48 * 1024 * 1024),
    )(*scalars, *inputs)


def spread_kernel(own_ref, out_ref):
    rows = []
    for image in range(2):
        cells = own_ref[image, 0].astype(F32)
        scale = lax.rsqrt(jnp.sum(cells * cells, axis=-1, keepdims=True) + NORM_EPS)
        rows.append(cells * scale)
    for part in range(4):
        for block in range(8):
            at = slice(part * 8, part * 8 + 8), slice(block * 128, block * 128 + 128)
            out_ref[part * 8 + block] = jnp.concatenate([rows[0][at], rows[1][at]], axis=0).astype(BF16)


def slots_kernel(src_ref, tgt_ref, slot_ref, slots_ref):
    for pair in range(src_ref.shape[0]):
        slots_ref[2 * pair] = slot_ref[src_ref[pair]]
        slots_ref[2 * pair + 1] = slot_ref[tgt_ref[pair]]


def select_kernel(slots_ref, held_ref, out_ref, pieces):
    groups = held_ref.shape[0]
    for group in range(groups):
        both = held_ref[group].astype(F32)
        pieces[2 * group] = both[:8]
        pieces[2 * group + 1] = both[8:]
    for group in range(groups):
        for pair in range(2):
            at = 4 * group + 2 * pair
            out_ref[group, pair] = jnp.concatenate(
                [pieces[slots_ref[at]], pieces[slots_ref[at + 1]]], axis=0
            ).astype(BF16)


def pack_kernel(chip_ref, held_ref, out_0, out_1, out_2, out_3):
    chip = chip_ref[0]
    for step, out_ref in enumerate((out_0, out_1, out_2, out_3)):
        pair = lax.rem(chip + step, CHIPS) // (CHIPS // 2)
        for group in range(held_ref.shape[0]):
            out_ref[group] = held_ref[group, pair]


def shifted(values, offset):
    amount = (-offset) % POS
    return pltpu.roll(values, amount, values.ndim - 1) if amount else values


def consensus_kernel(
    chip_ref, core_ref, own_0, own_1, own_2, own_3, oth_0, oth_1, oth_2, oth_3, z1_ref, z2_ref, z3_ref,
    keep_ref, give_ref, frame, src, tgt, x1, x2, h2, w3s, kept,
):
    chip = chip_ref[0]
    core = core_ref[0]
    for row in range(HGT):
        frame[row * FRAME : row * FRAME + 8] = jnp.zeros((8, frame.shape[1]), F32)
        frame[row * FRAME + 8 + WID : (row + 1) * FRAME] = jnp.zeros((8, frame.shape[1]), F32)
    for parity, gots in ((core, (own_0, own_1, own_2, own_3)), (1 - core, (oth_0, oth_1, oth_2, oth_3))):
        for step, got in enumerate(gots):
            row = 2 * lax.rem(chip + CHIPS - step, CHIPS) + parity
            for part in range(4):
                to_src = pl.ds(pl.multiple_of(row * FRAME + 8 + part * 8, 8), 8)
                to_tgt = pl.ds(pl.multiple_of(row * WID + part * 8, 8), 8)
                for block in range(8):
                    both = got[part * 8 + block].astype(F32)
                    frame[to_src, block * 128 : block * 128 + 128] = both[:8]
                    tgt[to_tgt, block * 128 : block * 128 + 128] = both[8:]
    for row in range(HGT):
        line = frame[pl.ds(pl.multiple_of(row * FRAME + BLOCK * core, 8), 32), :]
        src[row * 16 : row * 16 + 16] = line[4:20].astype(BF16)
        src[128 + row * 16 : 128 + row * 16 + 16] = line[12:28].astype(BF16)
    corr = lax.dot_general(
        src[...], tgt[...].astype(BF16), (((1,), (1,)), ((), ())), preferred_element_type=F32
    )
    corr = corr.astype(BF16).astype(F32)

    column = lax.broadcasted_iota(jnp.int32, (1, POS), 1)
    line = column // WID
    column = column % WID

    def col_mask(d):
        return ((column + d - 1 >= 0) & (column + d - 1 < WID)).astype(F32)

    def line_mask(c):
        return ((line + c - 1 >= 0) & (line + c - 1 < HGT)).astype(F32)

    has_left = (core > 0).astype(F32)
    has_right = (core < 1).astype(F32)

    z1 = z1_ref[...].astype(F32)
    w1 = [
        jnp.concatenate([pltpu.roll(z1, j + 2 * w, 1) if j + w else z1 for j in range(PART_1)], axis=0).astype(BF16)[:, :K_1]
        for w in range(2)
    ]
    z2 = z2_ref[...].astype(F32)
    rolled = [pltpu.roll(z2, CONV * j, 1) if j else z2 for j in range(PART_2)]
    w2 = jnp.concatenate(
        [rolled[j][k * CONV : k * CONV + CONV] for k in range(9) for j in range(PART_2)], axis=0
    ).astype(BF16)[:, :K_2]
    z3 = z3_ref[...].astype(F32)
    for j in range(PART_3):
        w3s[:, j, :] = pltpu.roll(z3, CONV * j, 1) if j else z3
    w3 = w3s[...].reshape(27 * PART_3, 256).astype(BF16)[:, :K_3]

    for c in range(3):
        for d in range(3):
            moved = (shifted(corr, WID * (c - 1) + d - 1) * (line_mask(c) * col_mask(d))).astype(BF16)
            for w in range(2):
                at = w * 160
                x1[c * 3 + d, at : at + 16] = jnp.zeros((16, POS), BF16)
                x1[c * 3 + d, at + 16 : at + 144] = moved[w * 128 : w * 128 + 128]
                x1[c * 3 + d, at + 144 : at + 160] = jnp.zeros((16, POS), BF16)
    left_mask, right_mask = col_mask(0), col_mask(2)
    for i in range(HGT):
        for w in range(2):
            at = w * 160 + 16 * i
            cells = jnp.concatenate([x1[k, at : at + 48] for k in range(9)], axis=0)
            hidden = jnp.maximum(jnp.dot(w1[w], cells, preferred_element_type=F32), 0.0)
            edge = 2 * CONV
            if w == 0:
                hidden = jnp.concatenate([hidden[:edge] * has_left, hidden[edge:]], axis=0)
            else:
                hidden = jnp.concatenate([hidden[: M_1 - edge], hidden[M_1 - edge :] * has_right], axis=0)
            at = i * ROWS_1 + w * M_1
            x2[0, at : at + M_1] = (shifted(hidden, -1) * left_mask).astype(BF16)
            x2[1, at : at + M_1] = hidden.astype(BF16)
            x2[2, at : at + M_1] = (shifted(hidden, 1) * right_mask).astype(BF16)

    up_mask, down_mask = line_mask(0), line_mask(2)
    for part in range(COLS_2 // PART_2):
        first = part * M_2
        rows = [None] * HGT
        for i in range(HGT):
            cells = jnp.concatenate([x2[d, i * ROWS_1 + first : i * ROWS_1 + first + K_PIECE] for d in range(3)], axis=0)
            low, high = (0 if i < HGT - 1 else 1), (3 if i > 0 else 2)
            parts = jnp.dot(w2[low * 3 * M_2 : high * 3 * M_2], cells, preferred_element_type=F32)
            for a in range(low, high):
                piece = parts[(a - low) * 3 * M_2 : (a - low + 1) * 3 * M_2]
                o = i + 1 - a
                rows[o] = piece if rows[o] is None else rows[o] + piece
            done = [i - 1] if i < HGT - 1 else [i - 1, i]
            for o in done:
                if o < 0:
                    continue
                total = rows[o][M_2 : 2 * M_2]
                total = total + shifted(rows[o][:M_2], -WID) * up_mask
                total = total + shifted(rows[o][2 * M_2 :], WID) * down_mask
                total = jnp.maximum(total, 0.0)
                if part == 0:
                    total = jnp.concatenate([total[:CONV] * has_left, total[CONV:]], axis=0)
                if part == COLS_2 // PART_2 - 1:
                    total = jnp.concatenate([total[: M_2 - CONV], total[M_2 - CONV :] * has_right], axis=0)
                h2[o, first : first + M_2] = total.astype(BF16)

    best = None
    sums = [[None] * HGT for _ in range(2)]
    for part in range(2):
        for i in range(HGT):
            parts = jnp.dot(w3, h2[i, part * 128 : part * 128 + K_3], preferred_element_type=F32)
            for a in range(3):
                o = i + 1 - a
                if 0 <= o < HGT:
                    piece = parts[a * 9 * PART_3 : (a + 1) * 9 * PART_3]
                    sums[part][o] = piece if sums[part][o] is None else sums[part][o] + piece
    for i in range(HGT):
        halves = []
        for part in range(2):
            total = None
            for c in range(3):
                for d in range(3):
                    k = (c * 3 + d) * PART_3
                    moved = shifted(sums[part][i][k : k + PART_3], WID * (c - 1) + d - 1) * (line_mask(c) * col_mask(d))
                    total = moved if total is None else total + moved
            halves.append(jnp.maximum(total, 0.0))
        total = jnp.concatenate(halves, axis=0)
        top = jnp.max(total, axis=0, keepdims=True)
        best = top if best is None else jnp.maximum(best, top)
        target_best = jnp.max(total, axis=1, keepdims=True)
        kept[i] = (total * (total / (target_best + EPSILON))).astype(BF16)
    pieces = []
    rest = best
    for _ in range(3):
        piece = rest.astype(BF16).astype(F32)
        pieces.append(piece)
        rest = rest - piece
    pieces = jnp.concatenate(pieces + [jnp.zeros((13, POS), F32)], axis=0).astype(BF16)
    far = CHIPS - 1 - chip
    for ref, parity in ((keep_ref, core), (give_ref, 1 - core)):
        ref[0] = kept[2 * chip + parity]
        ref[1] = kept[2 * far + parity]
        ref[2] = pieces


def consensus_scratch(channels):
    return (
        pltpu.VMEM((HGT * FRAME, channels), F32),
        pltpu.VMEM((2 * HGT * COLS_IN, channels), BF16),
        pltpu.VMEM((POS, channels), F32),
        pltpu.VMEM((9, 320, POS), BF16),
        pltpu.VMEM((3, HGT * ROWS_1, POS), BF16),
        pltpu.VMEM((HGT, ROWS_2, POS), BF16),
        pltpu.VMEM((27, PART_3, 256), F32),
        pltpu.VMEM((HGT, 16, POS), BF16),
    )


def finish_kernel(core_ref, keep_ref, got_ref, near_ref, far_ref, lines):
    core = core_ref[0]

    def largest(ref):
        top = ref[2].astype(F32)
        return top[0:1] + top[1:2] + top[2:3]

    best = jnp.maximum(largest(keep_ref), largest(got_ref)) + EPSILON
    for line in range(2):
        lines[line, core] = (keep_ref[line].astype(F32) / best).astype(BF16)
        lines[line, 1 - core] = (got_ref[line].astype(F32) / best).astype(BF16)
    near_ref[...] = lines[0]
    far_ref[...] = lines[1]


def place_kernel(chip_ref, near_ref, far_ref, out_ref):
    pair = chip_ref[0] // (CHIPS // 2)
    for half in range(2):
        out_ref[pair, 0, half * BLOCK : half * BLOCK + BLOCK] = near_ref[half]
        out_ref[1 - pair, 0, half * BLOCK : half * BLOCK + BLOCK] = far_ref[half]


def row_moves(chips, cores):
    return [(2 * y + c, 2 * ((y + chips) % CHIPS) + (c ^ cores)) for y in range(CHIPS) for c in range(2)]


def local(features, src_ids, tgt_ids, image_slot, w_first, w_mid, w_last):
    groups = lax.axis_size("pair")
    channels = features.shape[3]
    place = lax.axis_index("row").astype(jnp.int32)
    chip = (place // 2).reshape(1)
    core = (place % 2).reshape(1)

    tiles = call(spread_kernel, jax.ShapeDtypeStruct((groups, 16, 128), BF16), (features,))
    slots = call(
        slots_kernel,
        jax.ShapeDtypeStruct((2 * src_ids.shape[0],), jnp.int32),
        (),
        (src_ids, tgt_ids, image_slot),
        out_specs=whole(pltpu.SMEM),
    )
    held = lax.all_to_all(tiles, "pair", 0, 0, tiled=True)
    held, chip, core = lax.optimization_barrier((held, chip, core))
    wanted = call(
        select_kernel,
        jax.ShapeDtypeStruct((groups, 2, 16, 128), BF16),
        (held,),
        (slots,),
        (pltpu.VMEM((2 * groups, 8, 128), F32),),
    )
    routed = lax.all_to_all(wanted, "pair", 0, 0, tiled=True)
    routed, w_first, w_mid, w_last = lax.optimization_barrier((routed, w_first, w_mid, w_last))
    sends = call(pack_kernel, (jax.ShapeDtypeStruct((groups, 16, 128), BF16),) * 4, (routed,), (chip,))
    own = [sends[0]] + [lax.ppermute(sends[k], "row", row_moves(k, 0)) for k in range(1, CHIPS)]
    taps = w_first.reshape(3, 3, 3, 3, CONV).transpose(4, 2, 3, 0, 1)
    z1 = jnp.pad(taps, ((0, 0),) * 4 + ((1, COLS_IN - 4),)).reshape(CONV, K_1)
    z1 = jnp.pad(z1, ((0, 0), (0, 512 - K_1)))
    taps = w_mid.reshape(3, 3, 3, 3, CONV, CONV).transpose(0, 2, 4, 3, 1, 5)
    z2 = jnp.pad(taps, ((0, 0),) * 4 + ((0, PART_2 - 1), (0, 0))).reshape(9 * CONV, K_2)
    z2 = jnp.pad(z2, ((0, 0), (0, 256 - K_2)))
    z3 = w_last.reshape(3, 3, 3, 3, CONV).transpose(0, 2, 3, 1, 4).reshape(27, 3 * CONV)
    z3 = jnp.pad(z3, ((0, 0), (0, 256 - 3 * CONV)))
    own[1], z1, z2, z3 = lax.optimization_barrier((own[1], z1, z2, z3))
    other = [lax.ppermute(block, "row", row_moves(0, 1)) for block in own]
    message = jax.ShapeDtypeStruct((3, 16, POS), BF16)
    keep, give = call(
        consensus_kernel,
        (message, message),
        (*own, *other, z1, z2, z3),
        (chip, core),
        consensus_scratch(channels),
    )
    got = lax.ppermute(give, "row", row_moves(0, 1))
    lines = jax.ShapeDtypeStruct((2, BLOCK, POS), BF16)
    near, far = call(finish_kernel, (lines, lines), (keep, got), (core,), (pltpu.VMEM((2, 2, BLOCK, POS), BF16),))
    far = lax.ppermute(far, "row", [(2 * y + c, 2 * (CHIPS - 1 - y) + c) for y in range(CHIPS) for c in range(2)])
    return call(place_kernel, jax.ShapeDtypeStruct((2, 1, WID, POS), BF16), (near, far), (chip,))


def solution(mesh):
    placed = (P("pair", "row", None, None), P(), P(), P(), P(), P(), P())
    return jax.shard_map(
        local, mesh=mesh, in_specs=placed, out_specs=P("pair", "row", None, None), check_vma=False
    )
```

```python
import jax
import jax.numpy as jnp
from jax import lax
from jax.experimental import pallas as pl
from jax.experimental.pallas import tpu as pltpu
from jax.sharding import PartitionSpec as P

WID = 32
HGT = 8
POS = HGT * WID
CONV = 16
EPSILON = 1e-05
NORM_EPS = 1e-06
BF16 = jnp.bfloat16
F32 = jnp.float32

CHIPS = 4
BLOCK = WID // 2
COLS_IN = 16
PART_1 = 10
COLS_1, COLS_2 = BLOCK + 4, BLOCK + 2
PART_2 = 3
PART_3 = 8
ROWS_1, ROWS_2 = COLS_1 * CONV, COLS_2 * CONV
K_1 = 27 * COLS_IN
K_PIECE = (PART_2 + 2) * CONV
K_2 = 3 * K_PIECE
M_1 = PART_1 * CONV
M_2 = PART_2 * CONV
K_3 = (PART_3 + 2) * CONV
FRAME = WID + 16


def whole(space=pltpu.VMEM):
    return pl.BlockSpec(memory_space=space)


def call(kernel, out_shape, inputs, scalars=(), scratch=(), out_specs=None):
    return pl.pallas_call(
        kernel,
        out_shape=out_shape,
        in_specs=[whole(pltpu.SMEM)] * len(scalars) + [whole()] * len(inputs),
        out_specs=jax.tree.map(lambda _: whole(), out_shape) if out_specs is None else out_specs,
        scratch_shapes=list(scratch),
        compiler_params=pltpu.CompilerParams(vmem_limit_bytes=48 * 1024 * 1024),
    )(*scalars, *inputs)


def spread_kernel(own_ref, out_ref):
    rows = []
    for image in range(2):
        cells = own_ref[image, 0].astype(F32)
        scale = lax.rsqrt(jnp.sum(cells * cells, axis=-1, keepdims=True) + NORM_EPS)
        rows.append(cells * scale)
    for part in range(2):
        for block in range(8):
            at = slice(part * 8, part * 8 + 8), slice(block * 128, block * 128 + 128)
            out_ref[part * 8 + block] = jnp.concatenate([rows[0][at], rows[1][at]], axis=0).astype(BF16)


def slots_kernel(src_ref, tgt_ref, slot_ref, slots_ref):
    for pair in range(src_ref.shape[0]):
        slots_ref[2 * pair] = slot_ref[src_ref[pair]]
        slots_ref[2 * pair + 1] = slot_ref[tgt_ref[pair]]


def select_kernel(slots_ref, held_ref, out_ref, pieces):
    groups = held_ref.shape[0]
    for group in range(groups):
        both = held_ref[group].astype(F32)
        pieces[2 * group] = both[:8]
        pieces[2 * group + 1] = both[8:]
    for group in range(groups):
        for pair in range(2):
            at = 4 * group + 2 * pair
            out_ref[group, pair] = jnp.concatenate(
                [pieces[slots_ref[at]], pieces[slots_ref[at + 1]]], axis=0
            ).astype(BF16)


def pack_kernel(chip_ref, held_ref, out_0, out_1, out_2, out_3):
    chip = chip_ref[0]
    for step, out_ref in enumerate((out_0, out_1, out_2, out_3)):
        pair = lax.rem(chip + step, CHIPS) // (CHIPS // 2)
        for group in range(held_ref.shape[0]):
            out_ref[group] = held_ref[group, pair]


def shifted(values, offset):
    amount = (-offset) % POS
    return pltpu.roll(values, amount, values.ndim - 1) if amount else values


def consensus_kernel(
    chip_ref, core_ref, own_0, own_1, own_2, own_3, oth_0, oth_1, oth_2, oth_3, z1_ref, z2_ref, z3_ref,
    keep_ref, give_ref, frame, src, tgt, x1, x2, h2, w3s, kept,
):
    chip = chip_ref[0]
    core = core_ref[0]
    for row in range(HGT):
        frame[row * FRAME : row * FRAME + 8] = jnp.zeros((8, frame.shape[1]), F32)
        frame[row * FRAME + 8 + WID : (row + 1) * FRAME] = jnp.zeros((8, frame.shape[1]), F32)
    for parity, gots in ((core, (own_0, own_1, own_2, own_3)), (1 - core, (oth_0, oth_1, oth_2, oth_3))):
        for step, got in enumerate(gots):
            row = 2 * lax.rem(chip + CHIPS - step, CHIPS) + parity
            for part in range(4):
                to_src = pl.ds(pl.multiple_of(row * FRAME + 8 + part * 8, 8), 8)
                to_tgt = pl.ds(pl.multiple_of(row * WID + part * 8, 8), 8)
                for block in range(8):
                    both = got[part * 8 + block].astype(F32)
                    frame[to_src, block * 128 : block * 128 + 128] = both[:8]
                    tgt[to_tgt, block * 128 : block * 128 + 128] = both[8:]
    for row in range(HGT):
        line = frame[pl.ds(pl.multiple_of(row * FRAME + BLOCK * core, 8), 32), :]
        src[row * 16 : row * 16 + 16] = line[4:20].astype(BF16)
        src[128 + row * 16 : 128 + row * 16 + 16] = line[12:28].astype(BF16)
    corr = lax.dot_general(
        src[...], tgt[...].astype(BF16), (((1,), (1,)), ((), ())), preferred_element_type=F32
    )
    corr = corr.astype(BF16).astype(F32)

    column = lax.broadcasted_iota(jnp.int32, (1, POS), 1)
    line = column // WID
    column = column % WID

    def col_mask(d):
        return ((column + d - 1 >= 0) & (column + d - 1 < WID)).astype(F32)

    def line_mask(c):
        return ((line + c - 1 >= 0) & (line + c - 1 < HGT)).astype(F32)

    has_left = (core > 0).astype(F32)
    has_right = (core < 1).astype(F32)

    z1 = z1_ref[...].astype(F32)
    w1 = [
        jnp.concatenate([pltpu.roll(z1, j + 2 * w, 1) if j + w else z1 for j in range(PART_1)], axis=0).astype(BF16)[:, :K_1]
        for w in range(2)
    ]
    z2 = z2_ref[...].astype(F32)
    rolled = [pltpu.roll(z2, CONV * j, 1) if j else z2 for j in range(PART_2)]
    w2 = jnp.concatenate(
        [rolled[j][k * CONV : k * CONV + CONV] for k in range(9) for j in range(PART_2)], axis=0
    ).astype(BF16)[:, :K_2]
    z3 = z3_ref[...].astype(F32)
    for j in range(PART_3):
        w3s[:, j, :] = pltpu.roll(z3, CONV * j, 1) if j else z3
    w3 = w3s[...].reshape(27 * PART_3, 256).astype(BF16)[:, :K_3]

    for c in range(3):
        for d in range(3):
            moved = (shifted(corr, WID * (c - 1) + d - 1) * (line_mask(c) * col_mask(d))).astype(BF16)
            for w in range(2):
                at = w * 160
                x1[c * 3 + d, at : at + 16] = jnp.zeros((16, POS), BF16)
                x1[c * 3 + d, at + 16 : at + 144] = moved[w * 128 : w * 128 + 128]
                x1[c * 3 + d, at + 144 : at + 160] = jnp.zeros((16, POS), BF16)
    left_mask, right_mask = col_mask(0), col_mask(2)
    for i in range(HGT):
        for w in range(2):
            at = w * 160 + 16 * i
            cells = jnp.concatenate([x1[k, at : at + 48] for k in range(9)], axis=0)
            hidden = jnp.maximum(jnp.dot(w1[w], cells, preferred_element_type=F32), 0.0)
            edge = 2 * CONV
            if w == 0:
                hidden = jnp.concatenate([hidden[:edge] * has_left, hidden[edge:]], axis=0)
            else:
                hidden = jnp.concatenate([hidden[: M_1 - edge], hidden[M_1 - edge :] * has_right], axis=0)
            at = i * ROWS_1 + w * M_1
            x2[0, at : at + M_1] = (shifted(hidden, -1) * left_mask).astype(BF16)
            x2[1, at : at + M_1] = hidden.astype(BF16)
            x2[2, at : at + M_1] = (shifted(hidden, 1) * right_mask).astype(BF16)

    up_mask, down_mask = line_mask(0), line_mask(2)
    for part in range(COLS_2 // PART_2):
        first = part * M_2
        rows = [None] * HGT
        for i in range(HGT):
            cells = jnp.concatenate([x2[d, i * ROWS_1 + first : i * ROWS_1 + first + K_PIECE] for d in range(3)], axis=0)
            low, high = (0 if i < HGT - 1 else 1), (3 if i > 0 else 2)
            parts = jnp.dot(w2[low * 3 * M_2 : high * 3 * M_2], cells, preferred_element_type=F32)
            for a in range(low, high):
                piece = parts[(a - low) * 3 * M_2 : (a - low + 1) * 3 * M_2]
                o = i + 1 - a
                rows[o] = piece if rows[o] is None else rows[o] + piece
            done = [i - 1] if i < HGT - 1 else [i - 1, i]
            for o in done:
                if o < 0:
                    continue
                total = rows[o][M_2 : 2 * M_2]
                total = total + shifted(rows[o][:M_2], -WID) * up_mask
                total = total + shifted(rows[o][2 * M_2 :], WID) * down_mask
                total = jnp.maximum(total, 0.0)
                if part == 0:
                    total = jnp.concatenate([total[:CONV] * has_left, total[CONV:]], axis=0)
                if part == COLS_2 // PART_2 - 1:
                    total = jnp.concatenate([total[: M_2 - CONV], total[M_2 - CONV :] * has_right], axis=0)
                h2[o, first : first + M_2] = total.astype(BF16)

    best = None
    sums = [[None] * HGT for _ in range(2)]
    for part in range(2):
        for i in range(HGT):
            parts = jnp.dot(w3, h2[i, part * 128 : part * 128 + K_3], preferred_element_type=F32)
            for a in range(3):
                o = i + 1 - a
                if 0 <= o < HGT:
                    piece = parts[a * 9 * PART_3 : (a + 1) * 9 * PART_3]
                    sums[part][o] = piece if sums[part][o] is None else sums[part][o] + piece
    for i in range(HGT):
        halves = []
        for part in range(2):
            total = None
            for c in range(3):
                for d in range(3):
                    k = (c * 3 + d) * PART_3
                    moved = shifted(sums[part][i][k : k + PART_3], WID * (c - 1) + d - 1) * (line_mask(c) * col_mask(d))
                    total = moved if total is None else total + moved
            halves.append(jnp.maximum(total, 0.0))
        total = jnp.concatenate(halves, axis=0)
        top = jnp.max(total, axis=0, keepdims=True)
        best = top if best is None else jnp.maximum(best, top)
        target_best = jnp.max(total, axis=1, keepdims=True)
        kept[i] = (total * (total / (target_best + EPSILON))).astype(BF16)
    pieces = []
    rest = best
    for _ in range(3):
        piece = rest.astype(BF16).astype(F32)
        pieces.append(piece)
        rest = rest - piece
    pieces = jnp.concatenate(pieces + [jnp.zeros((13, POS), F32)], axis=0).astype(BF16)
    far = CHIPS - 1 - chip
    for ref, parity in ((keep_ref, core), (give_ref, 1 - core)):
        ref[0] = kept[2 * chip + parity]
        ref[1] = kept[2 * far + parity]
        ref[2] = pieces


def consensus_scratch(channels):
    return (
        pltpu.VMEM((HGT * FRAME, channels), F32),
        pltpu.VMEM((2 * HGT * COLS_IN, channels), BF16),
        pltpu.VMEM((POS, channels), F32),
        pltpu.VMEM((9, 320, POS), BF16),
        pltpu.VMEM((3, HGT * ROWS_1, POS), BF16),
        pltpu.VMEM((HGT, ROWS_2, POS), BF16),
        pltpu.VMEM((27, PART_3, 256), F32),
        pltpu.VMEM((HGT, 16, POS), BF16),
    )


def finish_kernel(core_ref, keep_ref, got_ref, near_ref, far_ref, lines):
    core = core_ref[0]

    def largest(ref):
        top = ref[2].astype(F32)
        return top[0:1] + top[1:2] + top[2:3]

    best = jnp.maximum(largest(keep_ref), largest(got_ref)) + EPSILON
    for line in range(2):
        lines[line, core] = (keep_ref[line].astype(F32) / best).astype(BF16)
        lines[line, 1 - core] = (got_ref[line].astype(F32) / best).astype(BF16)
    near_ref[...] = lines[0]
    far_ref[...] = lines[1]


def place_kernel(chip_ref, near_ref, far_ref, out_ref):
    pair = chip_ref[0] // (CHIPS // 2)
    for half in range(2):
        out_ref[pair, 0, half * BLOCK : half * BLOCK + BLOCK] = near_ref[half]
        out_ref[1 - pair, 0, half * BLOCK : half * BLOCK + BLOCK] = far_ref[half]


def row_moves(chips, cores):
    return [(2 * y + c, 2 * ((y + chips) % CHIPS) + (c ^ cores)) for y in range(CHIPS) for c in range(2)]


def local(features, src_ids, tgt_ids, image_slot, w_first, w_mid, w_last):
    groups = lax.axis_size("pair")
    channels = features.shape[3]
    place = lax.axis_index("row").astype(jnp.int32)
    chip = (place // 2).reshape(1)
    core = (place % 2).reshape(1)

    tiles = pl.pallas_call(
        spread_kernel,
        grid=(2,),
        out_shape=jax.ShapeDtypeStruct((groups, 16, 128), BF16),
        in_specs=[pl.BlockSpec((2, 1, WID // 2, channels), lambda half: (0, 0, half, 0))],
        out_specs=pl.BlockSpec((16, 16, 128), lambda half: (half, 0, 0)),
    )(features)
    slots = call(
        slots_kernel,
        jax.ShapeDtypeStruct((2 * src_ids.shape[0],), jnp.int32),
        (),
        (src_ids, tgt_ids, image_slot),
        out_specs=whole(pltpu.SMEM),
    )
    held = lax.all_to_all(tiles, "pair", 0, 0, tiled=True)
    held, chip, core = lax.optimization_barrier((held, chip, core))
    wanted = call(
        select_kernel,
        jax.ShapeDtypeStruct((groups, 2, 16, 128), BF16),
        (held,),
        (slots,),
        (pltpu.VMEM((2 * groups, 8, 128), F32),),
    )
    routed = lax.all_to_all(wanted, "pair", 0, 0, tiled=True)
    routed, w_first, w_mid, w_last = lax.optimization_barrier((routed, w_first, w_mid, w_last))
    sends = call(pack_kernel, (jax.ShapeDtypeStruct((groups, 16, 128), BF16),) * 4, (routed,), (chip,))
    own = [sends[0]] + [lax.ppermute(sends[k], "row", row_moves(k, 0)) for k in range(1, CHIPS)]
    taps = w_first.reshape(3, 3, 3, 3, CONV).transpose(4, 2, 3, 0, 1)
    z1 = jnp.pad(taps, ((0, 0),) * 4 + ((1, COLS_IN - 4),)).reshape(CONV, K_1)
    z1 = jnp.pad(z1, ((0, 0), (0, 512 - K_1)))
    taps = w_mid.reshape(3, 3, 3, 3, CONV, CONV).transpose(0, 2, 4, 3, 1, 5)
    z2 = jnp.pad(taps, ((0, 0),) * 4 + ((0, PART_2 - 1), (0, 0))).reshape(9 * CONV, K_2)
    z2 = jnp.pad(z2, ((0, 0), (0, 256 - K_2)))
    z3 = w_last.reshape(3, 3, 3, 3, CONV).transpose(0, 2, 3, 1, 4).reshape(27, 3 * CONV)
    z3 = jnp.pad(z3, ((0, 0), (0, 256 - 3 * CONV)))
    own[1], z1, z2, z3 = lax.optimization_barrier((own[1], z1, z2, z3))
    other = [lax.ppermute(block, "row", row_moves(0, 1)) for block in own]
    message = jax.ShapeDtypeStruct((3, 16, POS), BF16)
    keep, give = call(
        consensus_kernel,
        (message, message),
        (*own, *other, z1, z2, z3),
        (chip, core),
        consensus_scratch(channels),
    )
    got = lax.ppermute(give, "row", row_moves(0, 1))
    lines = jax.ShapeDtypeStruct((2, BLOCK, POS), BF16)
    near, far = call(finish_kernel, (lines, lines), (keep, got), (core,), (pltpu.VMEM((2, 2, BLOCK, POS), BF16),))
    far = lax.ppermute(far, "row", [(2 * y + c, 2 * (CHIPS - 1 - y) + c) for y in range(CHIPS) for c in range(2)])
    return call(place_kernel, jax.ShapeDtypeStruct((2, 1, WID, POS), BF16), (near, far), (chip,))


def solution(mesh):
    placed = (P("pair", "row", None, None), P(), P(), P(), P(), P(), P())
    return jax.shard_map(
        local, mesh=mesh, in_specs=placed, out_specs=P("pair", "row", None, None), check_vma=False
    )
```

```python
import jax
import jax.numpy as jnp
from jax import lax
from jax.experimental import pallas as pl
from jax.experimental.pallas import tpu as pltpu
from jax.sharding import PartitionSpec as P

WID = 32
HGT = 8
POS = HGT * WID
CONV = 16
EPSILON = 1e-05
NORM_EPS = 1e-06
BF16 = jnp.bfloat16
F32 = jnp.float32

CHIPS = 4
BLOCK = WID // 2
COLS_IN = 16
PART_1 = 10
COLS_1, COLS_2 = BLOCK + 4, BLOCK + 2
PART_2 = 3
PART_3 = 8
ROWS_1, ROWS_2 = COLS_1 * CONV, COLS_2 * CONV
K_1 = 27 * COLS_IN
K_PIECE = (PART_2 + 2) * CONV
K_2 = 3 * K_PIECE
M_1 = PART_1 * CONV
M_2 = PART_2 * CONV
K_3 = (PART_3 + 2) * CONV
FRAME = WID + 16


def whole(space=pltpu.VMEM):
    return pl.BlockSpec(memory_space=space)


def call(kernel, out_shape, inputs, scalars=(), scratch=(), out_specs=None):
    return pl.pallas_call(
        kernel,
        out_shape=out_shape,
        in_specs=[whole(pltpu.SMEM)] * len(scalars) + [whole()] * len(inputs),
        out_specs=jax.tree.map(lambda _: whole(), out_shape) if out_specs is None else out_specs,
        scratch_shapes=list(scratch),
        compiler_params=pltpu.CompilerParams(vmem_limit_bytes=48 * 1024 * 1024),
    )(*scalars, *inputs)


def spread_kernel(own_ref, out_ref):
    rows = []
    for image in range(2):
        cells = own_ref[image, 0].astype(F32)
        scale = lax.rsqrt(jnp.sum(cells * cells, axis=-1, keepdims=True) + NORM_EPS)
        rows.append(cells * scale)
    for part in range(2):
        for block in range(8):
            at = slice(part * 8, part * 8 + 8), slice(block * 128, block * 128 + 128)
            out_ref[part * 8 + block] = jnp.concatenate([rows[0][at], rows[1][at]], axis=0).astype(BF16)


def slots_kernel(src_ref, tgt_ref, slot_ref, slots_ref):
    batch = 16
    for first in range(0, src_ref.shape[0], batch):
        pairs = range(first, first + batch)
        ids = [ref[pair] for pair in pairs for ref in (src_ref, tgt_ref)]
        for place, slot in enumerate([slot_ref[image] for image in ids]):
            slots_ref[2 * first + place] = slot


def select_kernel(slots_ref, held_ref, out_ref, pieces):
    groups = held_ref.shape[0]
    for group in range(groups):
        both = held_ref[group].astype(F32)
        pieces[2 * group] = both[:8]
        pieces[2 * group + 1] = both[8:]
    for group in range(groups):
        for pair in range(2):
            at = 4 * group + 2 * pair
            out_ref[group, pair] = jnp.concatenate(
                [pieces[slots_ref[at]], pieces[slots_ref[at + 1]]], axis=0
            ).astype(BF16)


def pack_kernel(chip_ref, held_ref, out_0, out_1, out_2, out_3):
    chip = chip_ref[0]
    for step, out_ref in enumerate((out_0, out_1, out_2, out_3)):
        pair = lax.rem(chip + step, CHIPS) // (CHIPS // 2)
        for group in range(held_ref.shape[0]):
            out_ref[group] = held_ref[group, pair]


def shifted(values, offset):
    amount = (-offset) % POS
    return pltpu.roll(values, amount, values.ndim - 1) if amount else values


def consensus_kernel(
    chip_ref, core_ref, own_0, own_1, own_2, own_3, oth_0, oth_1, oth_2, oth_3, z1_ref, z2_ref, z3_ref,
    keep_ref, give_ref, frame, src, tgt, x1, x2, h2, w3s, kept,
):
    chip = chip_ref[0]
    core = core_ref[0]
    for row in range(HGT):
        frame[row * FRAME : row * FRAME + 8] = jnp.zeros((8, frame.shape[1]), F32)
        frame[row * FRAME + 8 + WID : (row + 1) * FRAME] = jnp.zeros((8, frame.shape[1]), F32)
    for parity, gots in ((core, (own_0, own_1, own_2, own_3)), (1 - core, (oth_0, oth_1, oth_2, oth_3))):
        for step, got in enumerate(gots):
            row = 2 * lax.rem(chip + CHIPS - step, CHIPS) + parity
            for part in range(4):
                to_src = pl.ds(pl.multiple_of(row * FRAME + 8 + part * 8, 8), 8)
                to_tgt = pl.ds(pl.multiple_of(row * WID + part * 8, 8), 8)
                for block in range(8):
                    both = got[part * 8 + block].astype(F32)
                    frame[to_src, block * 128 : block * 128 + 128] = both[:8]
                    tgt[to_tgt, block * 128 : block * 128 + 128] = both[8:]
    for row in range(HGT):
        line = frame[pl.ds(pl.multiple_of(row * FRAME + BLOCK * core, 8), 32), :]
        src[row * 16 : row * 16 + 16] = line[4:20].astype(BF16)
        src[128 + row * 16 : 128 + row * 16 + 16] = line[12:28].astype(BF16)
    corr = lax.dot_general(
        src[...], tgt[...].astype(BF16), (((1,), (1,)), ((), ())), preferred_element_type=F32
    )
    corr = corr.astype(BF16).astype(F32)

    column = lax.broadcasted_iota(jnp.int32, (1, POS), 1)
    line = column // WID
    column = column % WID

    def col_mask(d):
        return ((column + d - 1 >= 0) & (column + d - 1 < WID)).astype(F32)

    def line_mask(c):
        return ((line + c - 1 >= 0) & (line + c - 1 < HGT)).astype(F32)

    has_left = (core > 0).astype(F32)
    has_right = (core < 1).astype(F32)

    z1 = z1_ref[...].astype(F32)
    w1 = [
        jnp.concatenate([pltpu.roll(z1, j + 2 * w, 1) if j + w else z1 for j in range(PART_1)], axis=0).astype(BF16)[:, :K_1]
        for w in range(2)
    ]
    z2 = z2_ref[...].astype(F32)
    rolled = [pltpu.roll(z2, CONV * j, 1) if j else z2 for j in range(PART_2)]
    w2 = jnp.concatenate(
        [rolled[j][k * CONV : k * CONV + CONV] for k in range(9) for j in range(PART_2)], axis=0
    ).astype(BF16)[:, :K_2]
    z3 = z3_ref[...].astype(F32)
    for j in range(PART_3):
        w3s[:, j, :] = pltpu.roll(z3, CONV * j, 1) if j else z3
    w3 = w3s[...].reshape(27 * PART_3, 256).astype(BF16)[:, :K_3]

    for c in range(3):
        for d in range(3):
            moved = (shifted(corr, WID * (c - 1) + d - 1) * (line_mask(c) * col_mask(d))).astype(BF16)
            for w in range(2):
                at = w * 160
                x1[c * 3 + d, at : at + 16] = jnp.zeros((16, POS), BF16)
                x1[c * 3 + d, at + 16 : at + 144] = moved[w * 128 : w * 128 + 128]
                x1[c * 3 + d, at + 144 : at + 160] = jnp.zeros((16, POS), BF16)
    left_mask, right_mask = col_mask(0), col_mask(2)
    for i in range(HGT):
        for w in range(2):
            at = w * 160 + 16 * i
            cells = jnp.concatenate([x1[k, at : at + 48] for k in range(9)], axis=0)
            hidden = jnp.maximum(jnp.dot(w1[w], cells, preferred_element_type=F32), 0.0)
            edge = 2 * CONV
            if w == 0:
                hidden = jnp.concatenate([hidden[:edge] * has_left, hidden[edge:]], axis=0)
            else:
                hidden = jnp.concatenate([hidden[: M_1 - edge], hidden[M_1 - edge :] * has_right], axis=0)
            at = i * ROWS_1 + w * M_1
            x2[0, at : at + M_1] = (shifted(hidden, -1) * left_mask).astype(BF16)
            x2[1, at : at + M_1] = hidden.astype(BF16)
            x2[2, at : at + M_1] = (shifted(hidden, 1) * right_mask).astype(BF16)

    up_mask, down_mask = line_mask(0), line_mask(2)
    for part in range(COLS_2 // PART_2):
        first = part * M_2
        rows = [None] * HGT
        for i in range(HGT):
            cells = jnp.concatenate([x2[d, i * ROWS_1 + first : i * ROWS_1 + first + K_PIECE] for d in range(3)], axis=0)
            low, high = (0 if i < HGT - 1 else 1), (3 if i > 0 else 2)
            parts = jnp.dot(w2[low * 3 * M_2 : high * 3 * M_2], cells, preferred_element_type=F32)
            for a in range(low, high):
                piece = parts[(a - low) * 3 * M_2 : (a - low + 1) * 3 * M_2]
                o = i + 1 - a
                rows[o] = piece if rows[o] is None else rows[o] + piece
            done = [i - 1] if i < HGT - 1 else [i - 1, i]
            for o in done:
                if o < 0:
                    continue
                total = rows[o][M_2 : 2 * M_2]
                total = total + shifted(rows[o][:M_2], -WID) * up_mask
                total = total + shifted(rows[o][2 * M_2 :], WID) * down_mask
                total = jnp.maximum(total, 0.0)
                if part == 0:
                    total = jnp.concatenate([total[:CONV] * has_left, total[CONV:]], axis=0)
                if part == COLS_2 // PART_2 - 1:
                    total = jnp.concatenate([total[: M_2 - CONV], total[M_2 - CONV :] * has_right], axis=0)
                h2[o, first : first + M_2] = total.astype(BF16)

    best = None
    sums = [[None] * HGT for _ in range(2)]
    for part in range(2):
        for i in range(HGT):
            parts = jnp.dot(w3, h2[i, part * 128 : part * 128 + K_3], preferred_element_type=F32)
            for a in range(3):
                o = i + 1 - a
                if 0 <= o < HGT:
                    piece = parts[a * 9 * PART_3 : (a + 1) * 9 * PART_3]
                    sums[part][o] = piece if sums[part][o] is None else sums[part][o] + piece
    for i in range(HGT):
        halves = []
        for part in range(2):
            total = None
            for c in range(3):
                for d in range(3):
                    k = (c * 3 + d) * PART_3
                    moved = shifted(sums[part][i][k : k + PART_3], WID * (c - 1) + d - 1) * (line_mask(c) * col_mask(d))
                    total = moved if total is None else total + moved
            halves.append(jnp.maximum(total, 0.0))
        total = jnp.concatenate(halves, axis=0)
        top = jnp.max(total, axis=0, keepdims=True)
        best = top if best is None else jnp.maximum(best, top)
        target_best = jnp.max(total, axis=1, keepdims=True)
        kept[i] = (total * (total / (target_best + EPSILON))).astype(BF16)
    pieces = []
    rest = best
    for _ in range(3):
        piece = rest.astype(BF16).astype(F32)
        pieces.append(piece)
        rest = rest - piece
    pieces = jnp.concatenate(pieces + [jnp.zeros((13, POS), F32)], axis=0).astype(BF16)
    far = CHIPS - 1 - chip
    for ref, parity in ((keep_ref, core), (give_ref, 1 - core)):
        ref[0] = kept[2 * chip + parity]
        ref[1] = kept[2 * far + parity]
        ref[2] = pieces


def consensus_scratch(channels):
    return (
        pltpu.VMEM((HGT * FRAME, channels), F32),
        pltpu.VMEM((2 * HGT * COLS_IN, channels), BF16),
        pltpu.VMEM((POS, channels), F32),
        pltpu.VMEM((9, 320, POS), BF16),
        pltpu.VMEM((3, HGT * ROWS_1, POS), BF16),
        pltpu.VMEM((HGT, ROWS_2, POS), BF16),
        pltpu.VMEM((27, PART_3, 256), F32),
        pltpu.VMEM((HGT, 16, POS), BF16),
    )


def finish_kernel(core_ref, keep_ref, got_ref, near_ref, far_ref, lines):
    core = core_ref[0]

    def largest(ref):
        top = ref[2].astype(F32)
        return top[0:1] + top[1:2] + top[2:3]

    best = jnp.maximum(largest(keep_ref), largest(got_ref)) + EPSILON
    for line in range(2):
        lines[line, core] = (keep_ref[line].astype(F32) / best).astype(BF16)
        lines[line, 1 - core] = (got_ref[line].astype(F32) / best).astype(BF16)
    near_ref[...] = lines[0]
    far_ref[...] = lines[1]


def place_kernel(chip_ref, near_ref, far_ref, out_ref):
    pair = chip_ref[0] // (CHIPS // 2)
    for half in range(2):
        out_ref[pair, 0, half * BLOCK : half * BLOCK + BLOCK] = near_ref[half]
        out_ref[1 - pair, 0, half * BLOCK : half * BLOCK + BLOCK] = far_ref[half]


def row_moves(chips, cores):
    return [(2 * y + c, 2 * ((y + chips) % CHIPS) + (c ^ cores)) for y in range(CHIPS) for c in range(2)]


def local(features, src_ids, tgt_ids, image_slot, w_first, w_mid, w_last):
    groups = lax.axis_size("pair")
    channels = features.shape[3]
    place = lax.axis_index("row").astype(jnp.int32)
    chip = (place // 2).reshape(1)
    core = (place % 2).reshape(1)

    tiles = pl.pallas_call(
        spread_kernel,
        grid=(2,),
        out_shape=jax.ShapeDtypeStruct((groups, 16, 128), BF16),
        in_specs=[pl.BlockSpec((2, 1, WID // 2, channels), lambda half: (0, 0, half, 0))],
        out_specs=pl.BlockSpec((16, 16, 128), lambda half: (half, 0, 0)),
    )(features)
    slots = call(
        slots_kernel,
        jax.ShapeDtypeStruct((2 * src_ids.shape[0],), jnp.int32),
        (),
        (src_ids, tgt_ids, image_slot),
        out_specs=whole(pltpu.SMEM),
    )
    held = lax.all_to_all(tiles, "pair", 0, 0, tiled=True)
    taps = w_first.reshape(3, 3, 3, 3, CONV).transpose(4, 2, 3, 0, 1)
    z1 = jnp.pad(taps, ((0, 0),) * 4 + ((1, COLS_IN - 4),)).reshape(CONV, K_1)
    z1 = jnp.pad(z1, ((0, 0), (0, 512 - K_1)))
    z3 = w_last.reshape(3, 3, 3, 3, CONV).transpose(0, 2, 3, 1, 4).reshape(27, 3 * CONV)
    z3 = jnp.pad(z3, ((0, 0), (0, 256 - 3 * CONV)))
    held, chip, core, z1, z3 = lax.optimization_barrier((held, chip, core, z1, z3))
    wanted = call(
        select_kernel,
        jax.ShapeDtypeStruct((groups, 2, 16, 128), BF16),
        (held,),
        (slots,),
        (pltpu.VMEM((2 * groups, 8, 128), F32),),
    )
    routed = lax.all_to_all(wanted, "pair", 0, 0, tiled=True)
    routed, w_mid = lax.optimization_barrier((routed, w_mid))
    sends = call(pack_kernel, (jax.ShapeDtypeStruct((groups, 16, 128), BF16),) * 4, (routed,), (chip,))
    own = [sends[0]] + [lax.ppermute(sends[k], "row", row_moves(k, 0)) for k in range(1, CHIPS)]
    taps = w_mid.reshape(3, 3, 3, 3, CONV, CONV).transpose(0, 2, 4, 3, 1, 5)
    z2 = jnp.pad(taps, ((0, 0),) * 4 + ((0, PART_2 - 1), (0, 0))).reshape(9 * CONV, K_2)
    z2 = jnp.pad(z2, ((0, 0), (0, 256 - K_2)))
    own[1], z2 = lax.optimization_barrier((own[1], z2))
    other = [lax.ppermute(block, "row", row_moves(0, 1)) for block in own]
    message = jax.ShapeDtypeStruct((3, 16, POS), BF16)
    keep, give = call(
        consensus_kernel,
        (message, message),
        (*own, *other, z1, z2, z3),
        (chip, core),
        consensus_scratch(channels),
    )
    got = lax.ppermute(give, "row", row_moves(0, 1))
    lines = jax.ShapeDtypeStruct((2, BLOCK, POS), BF16)
    near, far = call(finish_kernel, (lines, lines), (keep, got), (core,), (pltpu.VMEM((2, 2, BLOCK, POS), BF16),))
    far = lax.ppermute(far, "row", [(2 * y + c, 2 * (CHIPS - 1 - y) + c) for y in range(CHIPS) for c in range(2)])
    return call(place_kernel, jax.ShapeDtypeStruct((2, 1, WID, POS), BF16), (near, far), (chip,))


def solution(mesh):
    placed = (P("pair", "row", None, None), P(), P(), P(), P(), P(), P())
    return jax.shard_map(
        local, mesh=mesh, in_specs=placed, out_specs=P("pair", "row", None, None), check_vma=False
    )
```

```python
import jax
import jax.numpy as jnp
from jax import lax
from jax.experimental import pallas as pl
from jax.experimental.pallas import tpu as pltpu
from jax.sharding import PartitionSpec as P

WID = 32
HGT = 8
POS = HGT * WID
CONV = 16
EPSILON = 1e-05
NORM_EPS = 1e-06
BF16 = jnp.bfloat16
F32 = jnp.float32

CHIPS = 4
BLOCK = WID // 2
COLS_IN = 16
PART_1 = 10
COLS_1, COLS_2 = BLOCK + 4, BLOCK + 2
PART_2 = 3
PART_3 = 8
ROWS_1, ROWS_2 = COLS_1 * CONV, COLS_2 * CONV
K_1 = 27 * COLS_IN
K_PIECE = (PART_2 + 2) * CONV
K_2 = 3 * K_PIECE
M_1 = PART_1 * CONV
M_2 = PART_2 * CONV
K_3 = (PART_3 + 2) * CONV
FRAME = WID + 16


def whole(space=pltpu.VMEM):
    return pl.BlockSpec(memory_space=space)


def call(kernel, out_shape, inputs, scalars=(), scratch=(), out_specs=None):
    return pl.pallas_call(
        kernel,
        out_shape=out_shape,
        in_specs=[whole(pltpu.SMEM)] * len(scalars) + [whole()] * len(inputs),
        out_specs=jax.tree.map(lambda _: whole(), out_shape) if out_specs is None else out_specs,
        scratch_shapes=list(scratch),
        compiler_params=pltpu.CompilerParams(vmem_limit_bytes=48 * 1024 * 1024),
    )(*scalars, *inputs)


def spread_kernel(own_ref, out_ref):
    rows = []
    for image in range(2):
        cells = own_ref[image, 0].astype(F32)
        scale = lax.rsqrt(jnp.sum(cells * cells, axis=-1, keepdims=True) + NORM_EPS)
        rows.append(cells * scale)
    for part in range(2):
        for block in range(8):
            at = slice(part * 8, part * 8 + 8), slice(block * 128, block * 128 + 128)
            out_ref[part * 8 + block] = jnp.concatenate([rows[0][at], rows[1][at]], axis=0).astype(BF16)


def slots_kernel(src_ref, tgt_ref, slot_ref, slots_ref):
    batch = 16
    for first in range(0, src_ref.shape[0], batch):
        pairs = range(first, first + batch)
        ids = [ref[pair] for pair in pairs for ref in (src_ref, tgt_ref)]
        for place, slot in enumerate([slot_ref[image] for image in ids]):
            slots_ref[2 * first + place] = slot


def select_kernel(slots_ref, held_ref, out_ref, pieces):
    groups = held_ref.shape[0]
    for group in range(groups):
        both = held_ref[group].astype(F32)
        pieces[2 * group] = both[:8]
        pieces[2 * group + 1] = both[8:]
    for group in range(groups):
        for pair in range(2):
            at = 4 * group + 2 * pair
            out_ref[group, pair] = jnp.concatenate(
                [pieces[slots_ref[at]], pieces[slots_ref[at + 1]]], axis=0
            ).astype(BF16)


def pack_kernel(chip_ref, held_ref, out_0, out_1, out_2, out_3):
    chip = chip_ref[0]
    for step, out_ref in enumerate((out_0, out_1, out_2, out_3)):
        pair = lax.rem(chip + step, CHIPS) // (CHIPS // 2)
        for group in range(held_ref.shape[0]):
            out_ref[group] = held_ref[group, pair]


def shifted(values, offset):
    amount = (-offset) % POS
    return pltpu.roll(values, amount, values.ndim - 1) if amount else values


def consensus_kernel(
    chip_ref, core_ref, own_0, own_1, own_2, own_3, oth_0, oth_1, oth_2, oth_3, z1_ref, z2_ref, z3_ref,
    keep_ref, give_ref, frame, src, tgt, x1, x2, h2, w3s, kept,
):
    chip = chip_ref[0]
    core = core_ref[0]
    for row in range(HGT):
        frame[row * FRAME : row * FRAME + 8] = jnp.zeros((8, frame.shape[1]), F32)
        frame[row * FRAME + 8 + WID : (row + 1) * FRAME] = jnp.zeros((8, frame.shape[1]), F32)
    for parity, gots in ((core, (own_0, own_1, own_2, own_3)), (1 - core, (oth_0, oth_1, oth_2, oth_3))):
        for step, got in enumerate(gots):
            row = 2 * lax.rem(chip + CHIPS - step, CHIPS) + parity
            for part in range(4):
                to_src = pl.ds(pl.multiple_of(row * FRAME + 8 + part * 8, 8), 8)
                to_tgt = pl.ds(pl.multiple_of(row * WID + part * 8, 8), 8)
                for block in range(8):
                    both = got[part * 8 + block].astype(F32)
                    frame[to_src, block * 128 : block * 128 + 128] = both[:8]
                    tgt[to_tgt, block * 128 : block * 128 + 128] = both[8:]
    for row in range(HGT):
        line = frame[pl.ds(pl.multiple_of(row * FRAME + BLOCK * core, 8), 32), :]
        src[row * 16 : row * 16 + 16] = line[4:20].astype(BF16)
        src[128 + row * 16 : 128 + row * 16 + 16] = line[12:28].astype(BF16)
    corr = lax.dot_general(
        src[...], tgt[...].astype(BF16), (((1,), (1,)), ((), ())), preferred_element_type=F32
    )
    corr = corr.astype(BF16).astype(F32)

    column = lax.broadcasted_iota(jnp.int32, (1, POS), 1)
    line = column // WID
    column = column % WID

    def col_mask(d):
        return ((column + d - 1 >= 0) & (column + d - 1 < WID)).astype(F32)

    def line_mask(c):
        return ((line + c - 1 >= 0) & (line + c - 1 < HGT)).astype(F32)

    has_left = (core > 0).astype(F32)
    has_right = (core < 1).astype(F32)

    z1 = z1_ref[...].astype(F32)
    w1 = [
        jnp.concatenate([pltpu.roll(z1, j + 2 * w, 1) if j + w else z1 for j in range(PART_1)], axis=0).astype(BF16)[:, :K_1]
        for w in range(2)
    ]
    z2 = z2_ref[...].astype(F32)
    rolled = [pltpu.roll(z2, CONV * j, 1) if j else z2 for j in range(PART_2)]
    w2 = jnp.concatenate(
        [rolled[j][k * CONV : k * CONV + CONV] for k in range(9) for j in range(PART_2)], axis=0
    ).astype(BF16)[:, :K_2]
    z3 = z3_ref[...].astype(F32)
    for j in range(PART_3):
        w3s[:, j, :] = pltpu.roll(z3, CONV * j, 1) if j else z3
    w3 = w3s[...].reshape(27 * PART_3, 256).astype(BF16)[:, :K_3]

    for c in range(3):
        for d in range(3):
            moved = (shifted(corr, WID * (c - 1) + d - 1) * (line_mask(c) * col_mask(d))).astype(BF16)
            for w in range(2):
                at = w * 160
                x1[c * 3 + d, at : at + 16] = jnp.zeros((16, POS), BF16)
                x1[c * 3 + d, at + 16 : at + 144] = moved[w * 128 : w * 128 + 128]
                x1[c * 3 + d, at + 144 : at + 160] = jnp.zeros((16, POS), BF16)
    left_mask, right_mask = col_mask(0), col_mask(2)
    for i in range(HGT):
        for w in range(2):
            at = w * 160 + 16 * i
            cells = jnp.concatenate([x1[k, at : at + 48] for k in range(9)], axis=0)
            hidden = jnp.maximum(jnp.dot(w1[w], cells, preferred_element_type=F32), 0.0)
            edge = 2 * CONV
            if w == 0:
                hidden = jnp.concatenate([hidden[:edge] * has_left, hidden[edge:]], axis=0)
            else:
                hidden = jnp.concatenate([hidden[: M_1 - edge], hidden[M_1 - edge :] * has_right], axis=0)
            at = i * ROWS_1 + w * M_1
            x2[0, at : at + M_1] = (shifted(hidden, -1) * left_mask).astype(BF16)
            x2[1, at : at + M_1] = hidden.astype(BF16)
            x2[2, at : at + M_1] = (shifted(hidden, 1) * right_mask).astype(BF16)

    up_mask, down_mask = line_mask(0), line_mask(2)
    for part in range(COLS_2 // PART_2):
        first = part * M_2
        rows = [None] * HGT
        for i in range(HGT):
            cells = jnp.concatenate([x2[d, i * ROWS_1 + first : i * ROWS_1 + first + K_PIECE] for d in range(3)], axis=0)
            low, high = (0 if i < HGT - 1 else 1), (3 if i > 0 else 2)
            parts = jnp.dot(w2[low * 3 * M_2 : high * 3 * M_2], cells, preferred_element_type=F32)
            for a in range(low, high):
                piece = parts[(a - low) * 3 * M_2 : (a - low + 1) * 3 * M_2]
                o = i + 1 - a
                rows[o] = piece if rows[o] is None else rows[o] + piece
            done = [i - 1] if i < HGT - 1 else [i - 1, i]
            for o in done:
                if o < 0:
                    continue
                total = rows[o][M_2 : 2 * M_2]
                total = total + shifted(rows[o][:M_2], -WID) * up_mask
                total = total + shifted(rows[o][2 * M_2 :], WID) * down_mask
                total = jnp.maximum(total, 0.0)
                if part == 0:
                    total = jnp.concatenate([total[:CONV] * has_left, total[CONV:]], axis=0)
                if part == COLS_2 // PART_2 - 1:
                    total = jnp.concatenate([total[: M_2 - CONV], total[M_2 - CONV :] * has_right], axis=0)
                h2[o, first : first + M_2] = total.astype(BF16)

    best = None
    sums = [[None] * HGT for _ in range(2)]
    for part in range(2):
        for i in range(HGT):
            parts = jnp.dot(w3, h2[i, part * 128 : part * 128 + K_3], preferred_element_type=F32)
            for a in range(3):
                o = i + 1 - a
                if 0 <= o < HGT:
                    piece = parts[a * 9 * PART_3 : (a + 1) * 9 * PART_3]
                    sums[part][o] = piece if sums[part][o] is None else sums[part][o] + piece
    for i in range(HGT):
        halves = []
        for part in range(2):
            total = None
            for c in range(3):
                for d in range(3):
                    k = (c * 3 + d) * PART_3
                    moved = shifted(sums[part][i][k : k + PART_3], WID * (c - 1) + d - 1) * (line_mask(c) * col_mask(d))
                    total = moved if total is None else total + moved
            halves.append(jnp.maximum(total, 0.0))
        total = jnp.concatenate(halves, axis=0)
        top = jnp.max(total, axis=0, keepdims=True)
        best = top if best is None else jnp.maximum(best, top)
        target_best = jnp.max(total, axis=1, keepdims=True)
        kept[i] = (total * (total / (target_best + EPSILON))).astype(BF16)
    pieces = []
    rest = best
    for _ in range(3):
        piece = rest.astype(BF16).astype(F32)
        pieces.append(piece)
        rest = rest - piece
    pieces = jnp.concatenate(pieces + [jnp.zeros((13, POS), F32)], axis=0).astype(BF16)
    far = CHIPS - 1 - chip
    for ref, parity in ((keep_ref, core), (give_ref, 1 - core)):
        ref[0] = kept[2 * chip + parity]
        ref[1] = kept[2 * far + parity]
        ref[2] = pieces


def consensus_scratch(channels):
    return (
        pltpu.VMEM((HGT * FRAME, channels), F32),
        pltpu.VMEM((2 * HGT * COLS_IN, channels), BF16),
        pltpu.VMEM((POS, channels), F32),
        pltpu.VMEM((9, 320, POS), BF16),
        pltpu.VMEM((3, HGT * ROWS_1, POS), BF16),
        pltpu.VMEM((HGT, ROWS_2, POS), BF16),
        pltpu.VMEM((27, PART_3, 256), F32),
        pltpu.VMEM((HGT, 16, POS), BF16),
    )


def finish_kernel(core_ref, keep_ref, got_ref, near_ref, far_ref, lines):
    core = core_ref[0]

    def largest(ref):
        top = ref[2].astype(F32)
        return top[0:1] + top[1:2] + top[2:3]

    best = jnp.maximum(largest(keep_ref), largest(got_ref)) + EPSILON
    for line in range(2):
        lines[line, core] = (keep_ref[line].astype(F32) / best).astype(BF16)
        lines[line, 1 - core] = (got_ref[line].astype(F32) / best).astype(BF16)
    near_ref[...] = lines[0]
    far_ref[...] = lines[1]


def place_kernel(chip_ref, near_ref, far_ref, out_ref):
    pair = chip_ref[0] // (CHIPS // 2)
    for half in range(2):
        out_ref[pair, 0, half * BLOCK : half * BLOCK + BLOCK] = near_ref[half]
        out_ref[1 - pair, 0, half * BLOCK : half * BLOCK + BLOCK] = far_ref[half]


def row_moves(chips, cores):
    return [(2 * y + c, 2 * ((y + chips) % CHIPS) + (c ^ cores)) for y in range(CHIPS) for c in range(2)]


def local(features, src_ids, tgt_ids, image_slot, w_first, w_mid, w_last):
    groups = lax.axis_size("pair")
    channels = features.shape[3]
    place = lax.axis_index("row").astype(jnp.int32)
    chip = (place // 2).reshape(1)
    core = (place % 2).reshape(1)

    tiles = pl.pallas_call(
        spread_kernel,
        grid=(2,),
        out_shape=jax.ShapeDtypeStruct((groups, 16, 128), BF16),
        in_specs=[pl.BlockSpec((2, 1, WID // 2, channels), lambda half: (0, 0, half, 0))],
        out_specs=pl.BlockSpec((16, 16, 128), lambda half: (half, 0, 0)),
    )(features)
    slots = call(
        slots_kernel,
        jax.ShapeDtypeStruct((2 * src_ids.shape[0],), jnp.int32),
        (),
        (src_ids, tgt_ids, image_slot),
        out_specs=whole(pltpu.SMEM),
    )
    held = lax.all_to_all(tiles, "pair", 0, 0, tiled=True)
    z3 = w_last.reshape(3, 3, 3, 3, CONV).transpose(0, 2, 3, 1, 4).reshape(27, 3 * CONV)
    z3 = jnp.pad(z3, ((0, 0), (0, 256 - 3 * CONV)))
    held, chip, core, z3 = lax.optimization_barrier((held, chip, core, z3))
    wanted = call(
        select_kernel,
        jax.ShapeDtypeStruct((groups, 2, 16, 128), BF16),
        (held,),
        (slots,),
        (pltpu.VMEM((2 * groups, 8, 128), F32),),
    )
    routed = lax.all_to_all(wanted, "pair", 0, 0, tiled=True)
    routed, w_first, w_mid = lax.optimization_barrier((routed, w_first, w_mid))
    sends = call(pack_kernel, (jax.ShapeDtypeStruct((groups, 16, 128), BF16),) * 4, (routed,), (chip,))
    own = [sends[0]] + [lax.ppermute(sends[k], "row", row_moves(k, 0)) for k in range(1, CHIPS)]
    taps = w_first.reshape(3, 3, 3, 3, CONV).transpose(4, 2, 3, 0, 1)
    z1 = jnp.pad(taps, ((0, 0),) * 4 + ((1, COLS_IN - 4),)).reshape(CONV, K_1)
    z1 = jnp.pad(z1, ((0, 0), (0, 512 - K_1)))
    taps = w_mid.reshape(3, 3, 3, 3, CONV, CONV).transpose(0, 2, 4, 3, 1, 5)
    z2 = jnp.pad(taps, ((0, 0),) * 4 + ((0, PART_2 - 1), (0, 0))).reshape(9 * CONV, K_2)
    z2 = jnp.pad(z2, ((0, 0), (0, 256 - K_2)))
    own[1], z1, z2 = lax.optimization_barrier((own[1], z1, z2))
    other = [lax.ppermute(block, "row", row_moves(0, 1)) for block in own]
    message = jax.ShapeDtypeStruct((3, 16, POS), BF16)
    keep, give = call(
        consensus_kernel,
        (message, message),
        (*own, *other, z1, z2, z3),
        (chip, core),
        consensus_scratch(channels),
    )
    got = lax.ppermute(give, "row", row_moves(0, 1))
    lines = jax.ShapeDtypeStruct((2, BLOCK, POS), BF16)
    near, far = call(finish_kernel, (lines, lines), (keep, got), (core,), (pltpu.VMEM((2, 2, BLOCK, POS), BF16),))
    far = lax.ppermute(far, "row", [(2 * y + c, 2 * (CHIPS - 1 - y) + c) for y in range(CHIPS) for c in range(2)])
    return call(place_kernel, jax.ShapeDtypeStruct((2, 1, WID, POS), BF16), (near, far), (chip,))


def solution(mesh):
    placed = (P("pair", "row", None, None), P(), P(), P(), P(), P(), P())
    return jax.shard_map(
        local, mesh=mesh, in_specs=placed, out_specs=P("pair", "row", None, None), check_vma=False
    )
```

```python
import jax
import jax.numpy as jnp
from jax import lax
from jax.experimental import pallas as pl
from jax.experimental.pallas import tpu as pltpu
from jax.sharding import PartitionSpec as P

WID = 32
HGT = 8
POS = HGT * WID
CONV = 16
EPSILON = 1e-05
NORM_EPS = 1e-06
BF16 = jnp.bfloat16
F32 = jnp.float32

CHIPS = 4
BLOCK = WID // 2
COLS_IN = 16
PART_1 = 10
COLS_1, COLS_2 = BLOCK + 4, BLOCK + 2
PART_2 = 3
PART_3 = 8
ROWS_1, ROWS_2 = COLS_1 * CONV, COLS_2 * CONV
K_1 = 27 * COLS_IN
K_PIECE = (PART_2 + 2) * CONV
K_2 = 3 * K_PIECE
M_1 = PART_1 * CONV
M_2 = PART_2 * CONV
K_3 = (PART_3 + 2) * CONV
FRAME = WID + 16


def whole(space=pltpu.VMEM):
    return pl.BlockSpec(memory_space=space)


def call(kernel, out_shape, inputs, scalars=(), scratch=(), out_specs=None):
    return pl.pallas_call(
        kernel,
        out_shape=out_shape,
        in_specs=[whole(pltpu.SMEM)] * len(scalars) + [whole()] * len(inputs),
        out_specs=jax.tree.map(lambda _: whole(), out_shape) if out_specs is None else out_specs,
        scratch_shapes=list(scratch),
        compiler_params=pltpu.CompilerParams(vmem_limit_bytes=48 * 1024 * 1024),
    )(*scalars, *inputs)


def spread_kernel(own_ref, out_ref):
    rows = []
    for image in range(2):
        cells = own_ref[image, 0].astype(F32)
        scale = lax.rsqrt(jnp.sum(cells * cells, axis=-1, keepdims=True) + NORM_EPS)
        rows.append(cells * scale)
    for part in range(2):
        for block in range(8):
            at = slice(part * 8, part * 8 + 8), slice(block * 128, block * 128 + 128)
            out_ref[part * 8 + block] = jnp.concatenate([rows[0][at], rows[1][at]], axis=0).astype(BF16)


def slots_kernel(src_ref, tgt_ref, slot_ref, slots_ref):
    batch = 16
    for first in range(0, src_ref.shape[0], batch):
        pairs = range(first, first + batch)
        ids = [ref[pair] for pair in pairs for ref in (src_ref, tgt_ref)]
        for place, slot in enumerate([slot_ref[image] for image in ids]):
            slots_ref[2 * first + place] = slot


def select_kernel(slots_ref, held_ref, out_ref, pieces):
    groups = held_ref.shape[0]
    for group in range(groups):
        both = held_ref[group].astype(F32)
        pieces[2 * group] = both[:8]
        pieces[2 * group + 1] = both[8:]
    for group in range(groups):
        for pair in range(2):
            at = 4 * group + 2 * pair
            out_ref[group, pair] = jnp.concatenate(
                [pieces[slots_ref[at]], pieces[slots_ref[at + 1]]], axis=0
            ).astype(BF16)


def pack_kernel(chip_ref, held_ref, out_0, out_1, out_2, out_3):
    chip = chip_ref[0]
    for step, out_ref in enumerate((out_0, out_1, out_2, out_3)):
        pair = lax.rem(chip + step, CHIPS) // (CHIPS // 2)
        for group in range(held_ref.shape[0]):
            out_ref[group] = held_ref[group, pair]


def shifted(values, offset):
    amount = (-offset) % POS
    return pltpu.roll(values, amount, values.ndim - 1) if amount else values


def consensus_kernel(
    chip_ref, core_ref, own_0, own_1, own_2, own_3, oth_0, oth_1, oth_2, oth_3, z1_ref, z2_ref, z3_ref,
    keep_ref, give_ref, frame, src, tgt, x1, x2, h2, w3s, kept,
):
    chip = chip_ref[0]
    core = core_ref[0]
    for row in range(HGT):
        frame[row * FRAME : row * FRAME + 8] = jnp.zeros((8, frame.shape[1]), F32)
        frame[row * FRAME + 8 + WID : (row + 1) * FRAME] = jnp.zeros((8, frame.shape[1]), F32)
    for parity, gots in ((core, (own_0, own_1, own_2, own_3)), (1 - core, (oth_0, oth_1, oth_2, oth_3))):
        for step, got in enumerate(gots):
            row = 2 * lax.rem(chip + CHIPS - step, CHIPS) + parity
            for part in range(4):
                to_src = pl.ds(pl.multiple_of(row * FRAME + 8 + part * 8, 8), 8)
                to_tgt = pl.ds(pl.multiple_of(row * WID + part * 8, 8), 8)
                for block in range(8):
                    both = got[part * 8 + block].astype(F32)
                    frame[to_src, block * 128 : block * 128 + 128] = both[:8]
                    tgt[to_tgt, block * 128 : block * 128 + 128] = both[8:]
    for row in range(HGT):
        line = frame[pl.ds(pl.multiple_of(row * FRAME + BLOCK * core, 8), 32), :]
        src[row * 16 : row * 16 + 16] = line[4:20].astype(BF16)
        src[128 + row * 16 : 128 + row * 16 + 16] = line[12:28].astype(BF16)
    corr = lax.dot_general(
        src[...], tgt[...].astype(BF16), (((1,), (1,)), ((), ())), preferred_element_type=F32
    )
    corr = corr.astype(BF16).astype(F32)

    column = lax.broadcasted_iota(jnp.int32, (1, POS), 1)
    line = column // WID
    column = column % WID

    def col_mask(d):
        return ((column + d - 1 >= 0) & (column + d - 1 < WID)).astype(F32)

    def line_mask(c):
        return ((line + c - 1 >= 0) & (line + c - 1 < HGT)).astype(F32)

    has_left = (core > 0).astype(F32)
    has_right = (core < 1).astype(F32)

    z1 = z1_ref[...].astype(F32)
    w1 = [
        jnp.concatenate([pltpu.roll(z1, j + 2 * w, 1) if j + w else z1 for j in range(PART_1)], axis=0).astype(BF16)[:, :K_1]
        for w in range(2)
    ]
    z2 = z2_ref[...].astype(F32)
    rolled = [pltpu.roll(z2, CONV * j, 1) if j else z2 for j in range(PART_2)]
    w2 = jnp.concatenate(
        [rolled[j][k * CONV : k * CONV + CONV] for k in range(9) for j in range(PART_2)], axis=0
    ).astype(BF16)[:, :K_2]
    z3 = z3_ref[...].astype(F32)
    for j in range(PART_3):
        w3s[:, j, :] = pltpu.roll(z3, CONV * j, 1) if j else z3
    w3 = w3s[...].reshape(27 * PART_3, 256).astype(BF16)[:, :K_3]

    for c in range(3):
        for d in range(3):
            moved = (shifted(corr, WID * (c - 1) + d - 1) * (line_mask(c) * col_mask(d))).astype(BF16)
            for w in range(2):
                at = w * 160
                x1[c * 3 + d, at : at + 16] = jnp.zeros((16, POS), BF16)
                x1[c * 3 + d, at + 16 : at + 144] = moved[w * 128 : w * 128 + 128]
                x1[c * 3 + d, at + 144 : at + 160] = jnp.zeros((16, POS), BF16)
    left_mask, right_mask = col_mask(0), col_mask(2)
    for i in range(HGT):
        for w in range(2):
            at = w * 160 + 16 * i
            cells = jnp.concatenate([x1[k, at : at + 48] for k in range(9)], axis=0)
            hidden = jnp.maximum(jnp.dot(w1[w], cells, preferred_element_type=F32), 0.0)
            edge = 2 * CONV
            if w == 0:
                hidden = jnp.concatenate([hidden[:edge] * has_left, hidden[edge:]], axis=0)
            else:
                hidden = jnp.concatenate([hidden[: M_1 - edge], hidden[M_1 - edge :] * has_right], axis=0)
            at = i * ROWS_1 + w * M_1
            x2[0, at : at + M_1] = (shifted(hidden, -1) * left_mask).astype(BF16)
            x2[1, at : at + M_1] = hidden.astype(BF16)
            x2[2, at : at + M_1] = (shifted(hidden, 1) * right_mask).astype(BF16)

    up_mask, down_mask = line_mask(0), line_mask(2)
    for part in range(COLS_2 // PART_2):
        first = part * M_2
        rows = [None] * HGT
        for i in range(HGT):
            cells = jnp.concatenate([x2[d, i * ROWS_1 + first : i * ROWS_1 + first + K_PIECE] for d in range(3)], axis=0)
            low, high = (0 if i < HGT - 1 else 1), (3 if i > 0 else 2)
            parts = jnp.dot(w2[low * 3 * M_2 : high * 3 * M_2], cells, preferred_element_type=F32)
            for a in range(low, high):
                piece = parts[(a - low) * 3 * M_2 : (a - low + 1) * 3 * M_2]
                o = i + 1 - a
                rows[o] = piece if rows[o] is None else rows[o] + piece
            done = [i - 1] if i < HGT - 1 else [i - 1, i]
            for o in done:
                if o < 0:
                    continue
                total = rows[o][M_2 : 2 * M_2]
                total = total + shifted(rows[o][:M_2], -WID) * up_mask
                total = total + shifted(rows[o][2 * M_2 :], WID) * down_mask
                total = jnp.maximum(total, 0.0)
                if part == 0:
                    total = jnp.concatenate([total[:CONV] * has_left, total[CONV:]], axis=0)
                if part == COLS_2 // PART_2 - 1:
                    total = jnp.concatenate([total[: M_2 - CONV], total[M_2 - CONV :] * has_right], axis=0)
                h2[o, first : first + M_2] = total.astype(BF16)

    best = None
    sums = [[None] * HGT for _ in range(2)]
    for part in range(2):
        for i in range(HGT):
            parts = jnp.dot(w3, h2[i, part * 128 : part * 128 + K_3], preferred_element_type=F32)
            for a in range(3):
                o = i + 1 - a
                if 0 <= o < HGT:
                    piece = parts[a * 9 * PART_3 : (a + 1) * 9 * PART_3]
                    sums[part][o] = piece if sums[part][o] is None else sums[part][o] + piece
    for i in range(HGT):
        halves = []
        for part in range(2):
            total = None
            for c in range(3):
                for d in range(3):
                    k = (c * 3 + d) * PART_3
                    moved = shifted(sums[part][i][k : k + PART_3], WID * (c - 1) + d - 1) * (line_mask(c) * col_mask(d))
                    total = moved if total is None else total + moved
            halves.append(jnp.maximum(total, 0.0))
        total = jnp.concatenate(halves, axis=0)
        top = jnp.max(total, axis=0, keepdims=True)
        best = top if best is None else jnp.maximum(best, top)
        target_best = jnp.max(total, axis=1, keepdims=True)
        kept[i] = (total * (total / (target_best + EPSILON))).astype(BF16)
    pieces = []
    rest = best
    for _ in range(3):
        piece = rest.astype(BF16).astype(F32)
        pieces.append(piece)
        rest = rest - piece
    pieces = jnp.concatenate(pieces + [jnp.zeros((13, POS), F32)], axis=0).astype(BF16)
    far = CHIPS - 1 - chip
    for ref, parity in ((keep_ref, core), (give_ref, 1 - core)):
        ref[0] = kept[2 * chip + parity]
        ref[1] = kept[2 * far + parity]
        ref[2] = pieces


def consensus_scratch(channels):
    return (
        pltpu.VMEM((HGT * FRAME, channels), F32),
        pltpu.VMEM((2 * HGT * COLS_IN, channels), BF16),
        pltpu.VMEM((POS, channels), F32),
        pltpu.VMEM((9, 320, POS), BF16),
        pltpu.VMEM((3, HGT * ROWS_1, POS), BF16),
        pltpu.VMEM((HGT, ROWS_2, POS), BF16),
        pltpu.VMEM((27, PART_3, 256), F32),
        pltpu.VMEM((HGT, 16, POS), BF16),
    )


def finish_kernel(core_ref, keep_ref, got_ref, near_ref, far_ref, lines):
    core = core_ref[0]

    def largest(ref):
        top = ref[2].astype(F32)
        return top[0:1] + top[1:2] + top[2:3]

    best = jnp.maximum(largest(keep_ref), largest(got_ref)) + EPSILON
    for line in range(2):
        lines[line, core] = (keep_ref[line].astype(F32) / best).astype(BF16)
        lines[line, 1 - core] = (got_ref[line].astype(F32) / best).astype(BF16)
    near_ref[...] = lines[0]
    far_ref[...] = lines[1]


def row_moves(chips, cores):
    return [(2 * y + c, 2 * ((y + chips) % CHIPS) + (c ^ cores)) for y in range(CHIPS) for c in range(2)]


def local(features, src_ids, tgt_ids, image_slot, w_first, w_mid, w_last):
    groups = lax.axis_size("pair")
    channels = features.shape[3]
    place = lax.axis_index("row").astype(jnp.int32)
    chip = (place // 2).reshape(1)
    core = (place % 2).reshape(1)

    tiles = pl.pallas_call(
        spread_kernel,
        grid=(2,),
        out_shape=jax.ShapeDtypeStruct((groups, 16, 128), BF16),
        in_specs=[pl.BlockSpec((2, 1, WID // 2, channels), lambda half: (0, 0, half, 0))],
        out_specs=pl.BlockSpec((16, 16, 128), lambda half: (half, 0, 0)),
    )(features)
    slots = call(
        slots_kernel,
        jax.ShapeDtypeStruct((2 * src_ids.shape[0],), jnp.int32),
        (),
        (src_ids, tgt_ids, image_slot),
        out_specs=whole(pltpu.SMEM),
    )
    held = lax.all_to_all(tiles, "pair", 0, 0, tiled=True)
    taps = w_first.reshape(3, 3, 3, 3, CONV).transpose(4, 2, 3, 0, 1)
    z1 = jnp.pad(taps, ((0, 0),) * 4 + ((1, COLS_IN - 4),)).reshape(CONV, K_1)
    z1 = jnp.pad(z1, ((0, 0), (0, 512 - K_1)))
    z3 = w_last.reshape(3, 3, 3, 3, CONV).transpose(0, 2, 3, 1, 4).reshape(27, 3 * CONV)
    z3 = jnp.pad(z3, ((0, 0), (0, 256 - 3 * CONV)))
    held, chip, core, z1, z3 = lax.optimization_barrier((held, chip, core, z1, z3))
    wanted = call(
        select_kernel,
        jax.ShapeDtypeStruct((groups, 2, 16, 128), BF16),
        (held,),
        (slots,),
        (pltpu.VMEM((2 * groups, 8, 128), F32),),
    )
    routed = lax.all_to_all(wanted, "pair", 0, 0, tiled=True)
    routed, w_mid = lax.optimization_barrier((routed, w_mid))
    sends = call(pack_kernel, (jax.ShapeDtypeStruct((groups, 16, 128), BF16),) * 4, (routed,), (chip,))
    own = [sends[0]] + [lax.ppermute(sends[k], "row", row_moves(k, 0)) for k in range(1, CHIPS)]
    taps = w_mid.reshape(3, 3, 3, 3, CONV, CONV).transpose(0, 2, 4, 3, 1, 5)
    z2 = jnp.pad(taps, ((0, 0),) * 4 + ((0, PART_2 - 1), (0, 0))).reshape(9 * CONV, K_2)
    z2 = jnp.pad(z2, ((0, 0), (0, 256 - K_2)))
    own[1], z2 = lax.optimization_barrier((own[1], z2))
    other = [lax.ppermute(block, "row", row_moves(0, 1)) for block in own]
    message = jax.ShapeDtypeStruct((3, 16, POS), BF16)
    keep, give = call(
        consensus_kernel,
        (message, message),
        (*own, *other, z1, z2, z3),
        (chip, core),
        consensus_scratch(channels),
    )
    got = lax.ppermute(give, "row", row_moves(0, 1))
    lines = jax.ShapeDtypeStruct((2, BLOCK, POS), BF16)
    near, far = call(finish_kernel, (lines, lines), (keep, got), (core,), (pltpu.VMEM((2, 2, BLOCK, POS), BF16),))
    far = lax.ppermute(far, "row", [(2 * y + c, 2 * (CHIPS - 1 - y) + c) for y in range(CHIPS) for c in range(2)])
    first = (chip < CHIPS // 2).reshape(1, 1, 1)
    return jnp.where(first, jnp.stack([near, far]), jnp.stack([far, near])).reshape(2, 1, WID, POS)


def solution(mesh):
    placed = (P("pair", "row", None, None), P(), P(), P(), P(), P(), P())
    return jax.shard_map(
        local, mesh=mesh, in_specs=placed, out_specs=P("pair", "row", None, None), check_vma=False
    )
```
